256 devices in a mesh: gz: 64 (over z, x, core), col: 4 (over y).
Axes of the slice: x: 4, y: 4, z: 8, core: 2. Of those that a mesh axis runs over, the one named last changes fastest.
Arguments:
- measured: float32 [736, 65536], P('col', 'gz'), may hold values from -6 to 6
- view_offset: int32 [1024], P('gz'), may hold values from 0 to 224, as said below
- tile_index: int32 [1024], P('gz'), may hold values from 0 to 7
- footprint: float32 [8, 64, 32], replicated, may hold values from -1 to 1
- transaxial: float32 [8, 736, 1024], P(None, 'col'), may hold values from -0.1875 to 0.1875
Outputs:
- volume: float32 [8192, 1024], P('gz', 'col')
- residual: float32 [736, 65536], P('col', 'gz')
- gradient: float32 [8192, 1024], P('gz', 'col')
The draws below stay inside these ranges and needn't reach their ends.
Inputs may be any that keep to these rules, and one draw needn't show every extreme that they name: `view_offset`: within each block of 16 views the offsets never fall; the block's first view has 0 and its last view has 224.
All inputs are finite; a program needn't handle non-finite values.
Results may differ from the reference program's by a relative error of at most 0.0003.
Values sent between devices are 32-bit elements; how exact they have to be, the bound alone decides.
A program may use at most 64 MiB of HBM per device.

```python
import jax
import jax.numpy as jnp
from jax import lax

NXW = 1024
C = 736
R = 64
NA = 8
NH = 8
ZW = 32
ITERS = 2
TURNS = 2
ZS = 128
HR = 64
WZ = 256
VB = 16
V = 1024
NZ = 8192
N_GZ = 64


def draw_view_offset(key, part):
    key = jax.random.fold_in(key, 7)
    steps = jax.random.randint(key, (N_GZ, VB), 1, 5)
    climb = jnp.cumsum(steps, axis=1) - steps[:, :1]
    summit = climb[:, -1:]
    return (climb * (WZ - ZW) // summit).reshape(-1).astype(jnp.int32)


def plant(entries, key, smallest, largest):
    dims = entries.shape
    index_at = [jax.random.randint(jax.random.fold_in(key, axis), (), 0, dims[axis]) for axis in range(len(dims))]
    entries = entries.at[tuple(index_at)].set(smallest)
    longest = dims.index(max(dims))
    index_at[longest] = (index_at[longest] + 1) % dims[longest]
    return entries.at[tuple(index_at)].set(largest)


def steps_of(own_key, shape, shards, least, high):
    level = 1.0
    for dim, blocks in shards:
        draws = jax.random.uniform(jax.random.fold_in(jax.random.fold_in(own_key, 6), dim), (blocks,), jnp.float32, least / len(shards), high / len(shards))
        level = level * jnp.repeat(jnp.exp(draws), shape[dim] // blocks).reshape((-1,) + (1,) * (len(shape) - 1 - dim))
    return level


def normal_values(rng, shape, scale, bound, cuts=(), held_as=jnp.bfloat16):
    array = jax.random.normal(rng, shape, jnp.float32) * scale
    if len(cuts) > 0:
        array = steps_of(rng, shape, cuts, -0.22, 0.18) * array
    return jnp.clip(array, min=-bound, max=bound).astype(held_as)


def setup_inputs(seed: int = 0) -> dict:
    key_list = jax.random.split(jax.random.key(seed), 6)
    return {
        "measured": normal_values(key_list[0], (C, V * R), 1.0, 6.0, ((0, 4), (1, 64)), jnp.float32),
        "view_offset": draw_view_offset(jax.random.fold_in(key_list[5], 71), 0),
        "tile_index": plant(jax.random.randint(key_list[2], (V,), 0, NH), jax.random.fold_in(key_list[2], 1), 0, NH - 1).astype(jnp.int32),
        "footprint": normal_values(key_list[3], (NH, R, ZW), ZW ** -0.5, 1.0, (), jnp.float32),
        "transaxial": normal_values(key_list[4], (NA, C, NXW), NXW ** -0.5, 0.1875, ((1, 4),), jnp.float32),
    }


def block_forward(window, offsets, tiles, transaxial):
    index = offsets[:, None] + jnp.arange(ZW, dtype=jnp.int32)[None, :]
    picked = window[index]
    projected = jnp.einsum('vrj,vjx->vrx', tiles, picked, precision=lax.Precision.HIGHEST)
    sinogram = jnp.einsum('tarx,acx->ctar', projected.reshape(TURNS, NA, R, NXW), transaxial, precision=lax.Precision.HIGHEST)
    return sinogram.reshape(C, VB * R)


def block_adjoint(data, offsets, tiles, transaxial):
    index = offsets[:, None] + jnp.arange(ZW, dtype=jnp.int32)[None, :]
    spread_cols = jnp.einsum('ctar,acx->tarx', data.reshape(C, TURNS, NA, R), transaxial, precision=lax.Precision.HIGHEST)
    spread = jnp.einsum('vrj,vrx->vjx', tiles, spread_cols.reshape(VB, R, NXW), precision=lax.Precision.HIGHEST)
    return jnp.zeros((WZ, NXW), jnp.float32).at[index].add(spread)


def reference(measured, view_offset, tile_index, footprint, transaxial):
    offsets = view_offset.reshape(N_GZ, VB)
    tiles = footprint[tile_index].reshape(N_GZ, VB, R, ZW)
    starts = (jnp.arange(N_GZ, dtype=jnp.int32) * ZS).astype(jnp.int32)

    def forward(field):
        padded = jnp.pad(field, ((HR, HR), (0, 0)))

        def one_block(items):
            start, offs, tile_block = items
            window = lax.dynamic_slice_in_dim(padded, start, WZ, 0)
            return block_forward(window, offs, tile_block, transaxial)

        blocks = lax.map(one_block, (starts, offsets, tiles))
        return jnp.transpose(blocks, (1, 0, 2)).reshape(C, V * R)

    def adjoint(data):
        def one_block(items):
            offs, tile_block, block_data = items
            return block_adjoint(block_data, offs, tile_block, transaxial)

        block_data = jnp.transpose(data.reshape(C, N_GZ, VB * R), (1, 0, 2))
        pieces = lax.map(one_block, (offsets, tiles, block_data))

        def accumulate(block, total):
            start = (block * ZS).astype(jnp.int32)
            current = lax.dynamic_slice_in_dim(total, start, WZ, 0)
            return lax.dynamic_update_slice_in_dim(total, current + pieces[block], start, 0)

        padded = lax.fori_loop(0, N_GZ, accumulate, jnp.zeros((NZ + 2 * HR, NXW), jnp.float32))
        return padded[HR:HR + NZ]

    volume = jnp.zeros((NZ, NXW), jnp.float32)
    residual = measured
    gradient = adjoint(residual)
    step_dir = gradient
    grad_norm = jnp.sum(gradient * gradient)
    for sweep in range(ITERS):
        image = forward(step_dir)
        step_size = grad_norm / jnp.sum(image * image)
        volume = volume + step_size * step_dir
        residual = residual - step_size * image
        gradient = adjoint(residual)
        if sweep + 1 < ITERS:
            next_norm = jnp.sum(gradient * gradient)
            step_dir = gradient + (next_norm / grad_norm) * step_dir
            grad_norm = next_norm
    return volume, residual, gradient
```

```python
import functools

import jax
import jax.numpy as jnp
from jax import lax
from jax.experimental import pallas as pl
from jax.experimental.pallas import tpu as pltpu
from jax.sharding import PartitionSpec as P

MESH = pl.DeviceIdType.MESH
F32 = jnp.float32
BF16 = jnp.bfloat16

NA = 8
R = 64
ZW = 32
ZS = 128
HR = 64
WZ = 256
C = 184
NXW = 1024
NCOL = 4
VX = NXW // NCOL
PAIRS = NA // 2
PW = 384
KC = PAIRS * PW
TOP = WZ - ZW
NT = (((1,), (1,)), ((), ()))
NN = (((1,), (0,)), ((), ()))


def split(x):
    hi = x.astype(BF16)
    return hi, (x - hi.astype(F32)).astype(BF16)


def dot3(a_hi, a_lo, b_hi, b_lo, dims):
    dot = functools.partial(lax.dot_general, dimension_numbers=dims, preferred_element_type=F32)
    return dot(a_hi, b_hi) + (dot(a_lo, b_hi) + dot(a_hi, b_lo))


def squares(x):
    rows, lanes = x.shape
    y = jnp.sum((x * x).reshape(rows // 8, 8, lanes), axis=0)
    return sum(y[:, k * 128 : (k + 1) * 128] for k in range(lanes // 128))


def kernel(
    lo_size,
    off_ref, tile_ref, foot_ref, meas_ref, trans_ref,
    vol_ref, res_ref, grad_ref,
    stage, t_hi, t_lo, fpad, shifted, w_hi, w_lo, wt_hi, wt_lo,
    z_hi, z_lo, q_main, q_rim, q0, q1, r1,
    part, rim_lo, rim_hi, relay, direct,
    window, g0, g1, d1,
    ar1, ar2, ar3,
    t_sem, b_send, b_recv, a_send, a_recv, ar_send, ar_recv,
):
    n_gz = lax.axis_size("gz")
    hi_size = n_gz // lo_size
    gz = lax.axis_index("gz")
    y = lax.axis_index("col")
    z_at = lax.div(gz, lo_size)
    lo_at = lax.rem(gz, lo_size)
    above = lax.rem(gz + 1, n_gz)
    below = lax.rem(gz + n_gz - 1, n_gz)
    nxt = lax.rem(y + 1, NCOL)
    prv = lax.rem(y + NCOL - 1, NCOL)

    def col_peer(d):
        return (gz, lax.rem(y + d, NCOL))

    def lo_peer(d):
        return (z_at * lo_size + lax.rem(lo_at + d, lo_size), y)

    def hi_peer(d):
        return (lax.rem(z_at + d, hi_size) * lo_size + lo_at, y)

    groups = ((NCOL, col_peer), (lo_size, lo_peer), (hi_size, hi_peer))

    barrier = pltpu.get_barrier_semaphore()
    count = 0
    for size, peer in groups:
        for d in range(1, size):
            pl.semaphore_signal(barrier, inc=1, device_id=peer(d), device_id_type=MESH)
            count += 1
    for other in (above, below):
        pl.semaphore_signal(barrier, inc=1, device_id=(other, y), device_id_type=MESH)
        count += 1

    loads = [pltpu.make_async_copy(trans_ref.at[a], stage.at[a], t_sem.at[a]) for a in range(NA)]
    for load in loads:
        load.start()

    lane = lax.broadcasted_iota(jnp.int32, (1, 128), 1)
    first_half = lane < 64

    fpad[...] = jnp.zeros_like(fpad)
    shifted[...] = jnp.zeros_like(shifted)

    def place(a, _):
        fpad[0:R, 0:ZW] = foot_ref[tile_ref[a]]
        fpad[R : 2 * R, 0:ZW] = foot_ref[tile_ref[a + NA]]
        shifted[TOP:WZ, :] = jnp.transpose(fpad[...])[0:ZW]
        one = shifted[pl.ds(TOP - off_ref[a], WZ), :]
        two = shifted[pl.ds(TOP - off_ref[a + NA], WZ), :]
        w = jnp.where(first_half, one, two)
        hi, lo = split(w)
        w_hi[a] = hi
        w_lo[a] = lo
        hi, lo = split(jnp.transpose(w))
        wt_hi[a] = hi
        wt_lo[a] = lo
        return 0

    lax.fori_loop(0, NA, place, 0)

    def put_z(p, za, zb):
        third = jnp.where(first_half, za[:, 128:], zb[:, 128:])
        hi, lo = split(jnp.concatenate([za[:, :128], zb[:, :128], third], axis=1))
        at = pl.ds(pl.multiple_of(p * PW, 128), PW)
        z_hi[:, at] = hi
        z_lo[:, at] = lo

    def z_of_measured(p, _):
        x = meas_ref[:, pl.ds(pl.multiple_of(p * 128, 128), 128)]
        v = meas_ref[:, pl.ds(pl.multiple_of(512 + p * 128, 128), 128)]
        ma = jnp.where(first_half, x, pltpu.roll(v, 64, 1))
        mb = jnp.where(first_half, pltpu.roll(x, 64, 1), v)
        ma = jnp.concatenate([ma, jnp.zeros((72, 128), F32)], axis=0)
        mb = jnp.concatenate(
            [mb[:128], jnp.zeros((64, 128), F32), mb[128:], jnp.zeros((8, 128), F32)], axis=0
        )
        za = dot3(w_hi[2 * p], w_lo[2 * p], *split(ma), NT)
        zb = dot3(w_hi[2 * p + 1], w_lo[2 * p + 1], *split(mb), NT)
        put_z(p, za, zb)
        return 0

    def z_of(p, x):
        hi, lo = split(x)
        pick = lambda v, k: jnp.concatenate([v[:, k * 128 : (k + 1) * 128], v[:, 256:]], axis=1)
        za = dot3(w_hi[2 * p], w_lo[2 * p], pick(hi, 0), pick(lo, 0), NN)
        zb = dot3(w_hi[2 * p + 1], w_lo[2 * p + 1], pick(hi, 1), pick(lo, 1), NN)
        put_z(p, za, zb)

    lax.fori_loop(0, PAIRS, z_of_measured, 0)

    def convert(p, _):
        for h in range(2):
            a = 2 * p + h
            pltpu.make_async_copy(trans_ref.at[a], stage.at[a], t_sem.at[a]).wait()
        base = p * PW
        for s in range(NCOL):
            cols = slice(s * VX, (s + 1) * VX)
            for h in range(2):
                a = 2 * p + h
                hi, lo = split(stage[a, 0:128, cols])
                at = pl.ds(pl.multiple_of(base + h * 128, 64), 128)
                t_hi[s, at] = hi
                t_lo[s, at] = lo
                tail = jnp.concatenate([stage[a, 128:C, cols], jnp.zeros((8, VX), F32)], axis=0)
                hi, lo = split(tail)
                at = pl.ds(pl.multiple_of(base + 256 + h * 64, 64), 64)
                t_hi[s, at] = hi
                t_lo[s, at] = lo
        return 0

    lax.fori_loop(0, PAIRS, convert, 0)

    pl.semaphore_wait(barrier, count)

    def remote(src, dst, send, recv, to):
        return pltpu.make_async_remote_copy(
            src_ref=src, dst_ref=dst, send_sem=send, recv_sem=recv, device_id=to, device_id_type=MESH
        )

    ar_bufs = (ar1, ar2, ar3)
    ar_at = (y, lo_at, z_at)
    ar_base = (0, NCOL, NCOL + lo_size)

    def ar_copy(k, level, d):
        size, peer = groups[level]
        slot = ar_bufs[level].at[k, ar_at[level]]
        return remote(
            slot, slot, ar_send.at[k, ar_base[level] + d], ar_recv.at[k, ar_base[level] + d], peer(d)
        )

    def ar_put(k, level, value):
        ar_bufs[level][k, ar_at[level]] = value

        def go(d, _):
            ar_copy(k, level, d).start()
            return 0

        lax.fori_loop(1, groups[level][0], go, 0)

    def ar_get(k, level):
        def done(d, _):
            ar_copy(k, level, d).wait()
            return 0

        lax.fori_loop(1, groups[level][0], done, 0)
        return jnp.sum(ar_bufs[level][k], axis=0)

    def b_rim(phase, i, side):
        rows = slice(WZ - HR, WZ) if side == 0 else slice(0, HR)
        to = above if side == 0 else below
        buf = rim_lo if side == 0 else rim_hi
        return remote(
            part.at[phase, i, rows], buf.at[phase, i],
            b_send.at[phase, 2 * i + side], b_recv.at[phase, 2 * i + side], (to, y),
        )

    def half(h):
        return slice(HR + h * 64, HR + h * 64 + 64)

    def b_relay(phase, h):
        return remote(
            part.at[phase, 0, half(h)], relay.at[phase, h],
            b_send.at[phase, 8 + h], b_recv.at[phase, 8 + h], (gz, nxt if h == 0 else prv),
        )

    def b_direct(phase, side, h):
        k = 10 + 2 * side + h
        return remote(
            part.at[phase, 1 + side, half(h)], direct.at[phase, side, h],
            b_send.at[phase, k], b_recv.at[phase, k], (gz, nxt if side == 0 else prv),
        )

    def with_rim(phase, i, h):
        b_rim(phase, i, h).wait_recv()
        if h == 0:
            rim = jnp.where(gz > 0, rim_lo[phase, i], 0.0)
        else:
            rim = jnp.where(gz < n_gz - 1, rim_hi[phase, i], 0.0)
        return part[phase, i, half(h)] + rim

    def back(phase, beside=()):
        beside = list(beside) + [lambda: None] * (4 - len(beside))

        def product(i, _):
            s = lax.rem(y + 2 + 3 * i + 3 * lax.div(i * (i - 1), 2), NCOL)
            part[phase, i] = dot3(z_hi[...], z_lo[...], t_hi[s], t_lo[s], NN)
            b_rim(phase, i, 0).start()
            b_rim(phase, i, 1).start()
            return 0

        lax.fori_loop(0, NCOL, product, 0)
        for h in range(2):
            part[phase, 0, half(h)] = with_rim(phase, 0, h)
            b_relay(phase, h).start()
        beside[0]()
        for side in range(2):
            h = 1 - side
            part[phase, 1 + side, half(h)] = with_rim(phase, 1 + side, h)
            b_direct(phase, side, h).start()
        beside[1]()
        for side in range(2):
            h = side
            own = with_rim(phase, 1 + side, h)
            b_relay(phase, h).wait_recv()
            part[phase, 1 + side, half(h)] = own + relay[phase, h]
            b_direct(phase, side, h).start()
        beside[2]()
        halves = [with_rim(phase, 3, h) for h in range(2)]
        for h in range(2):
            for side in range(2):
                b_direct(phase, side, h).wait_recv()
        beside[3]()
        return jnp.concatenate(
            [halves[h] + (direct[phase, 0, h] + direct[phase, 1, h]) for h in range(2)], axis=0
        )

    def a_main(phase, side, h):
        k = 2 * side + h
        return remote(
            window.at[phase, 0, half(h)], window.at[phase, 1 + side, half(h)],
            a_send.at[phase, k], a_recv.at[phase, k], (gz, nxt if side == 0 else prv),
        )

    def a_forward(phase, h):
        k = 4 + h
        return remote(
            window.at[phase, 1 + h, half(h)], window.at[phase, 3, half(h)],
            a_send.at[phase, k], a_recv.at[phase, k], (gz, nxt if h == 0 else prv),
        )

    def a_rim(phase, i, h):
        k = 6 + 2 * i + h
        rows = slice(WZ - HR, WZ) if h == 0 else slice(0, HR)
        return remote(
            window.at[phase, i, half(h)], window.at[phase, i, rows],
            a_send.at[phase, k], a_recv.at[phase, k], (below if h == 0 else above, y),
        )

    def gather_into(target, i, x, first):
        s = lax.rem(y + 3 * i + 3 * ((i * (i - 1)) // 2), NCOL)
        hi, lo = split(x)

        def part_of(n, _):
            at = pl.ds(pl.multiple_of(n * 512, 512), 512)
            value = dot3(hi, lo, t_hi[s, at], t_lo[s, at], NT)
            if first:
                target[:, at] = value
            else:
                target[:, at] += value
            return 0

        lax.fori_loop(0, KC // 512, part_of, 0)

    def forward(phase, field, beside=()):
        beside = list(beside) + [lambda: None] * (4 - len(beside))
        window[phase, 0, HR : HR + ZS] = field
        a_main(phase, 0, 0).start()
        a_main(phase, 1, 1).start()
        a_main(phase, 0, 1).start()
        a_main(phase, 1, 0).start()
        a_rim(phase, 0, 0).start()
        a_rim(phase, 0, 1).start()
        gather_into(q_main, 0, field, True)
        beside[0]()
        for h in range(2):
            a_main(phase, h, h).wait_recv()
            a_forward(phase, h).start()
            a_rim(phase, 1 + h, h).start()
        for h in range(2):
            a_main(phase, h, 1 - h).wait_recv()
            a_rim(phase, 1 + h, 1 - h).start()
        for side in range(2):
            gather_into(q_main, 1 + side, window[phase, 1 + side, HR : HR + ZS], False)
        beside[1]()
        for h in range(2):
            a_forward(phase, h).wait_recv()
            a_rim(phase, 3, h).start()
        gather_into(q_main, 3, window[phase, 3, HR : HR + ZS], False)
        beside[2]()
        for i in range(NCOL):
            for h in range(2):
                a_rim(phase, i, h).wait_recv()
            low = jnp.where(gz > 0, window[phase, i, 0:HR], 0.0)
            high = jnp.where(gz < n_gz - 1, window[phase, i, WZ - HR : WZ], 0.0)
            gather_into(q_rim, i, jnp.concatenate([low, high], axis=0), i == 0)
        beside[3]()

    def rays(p):
        at = pl.ds(pl.multiple_of(p * PW, 128), PW)
        full = jnp.concatenate([q_rim[0:HR, at], q_main[:, at], q_rim[HR:, at]], axis=0)
        hi, lo = split(full)
        pick = lambda v, k: jnp.concatenate([v[:, k * 128 : (k + 1) * 128], v[:, 256:]], axis=1)
        pa = dot3(wt_hi[2 * p], wt_lo[2 * p], pick(hi, 0), pick(lo, 0), NN)
        pb = dot3(wt_hi[2 * p + 1], wt_lo[2 * p + 1], pick(hi, 1), pick(lo, 1), NN)
        third = jnp.where(first_half, pa[:, 128:], pb[:, 128:])
        return jnp.concatenate([pa[:, :128], pb[:, :128], third], axis=1)

    def to_columns(x):
        x0, x1, x2 = (jnp.transpose(x[:, k * 128 : (k + 1) * 128]) for k in range(3))
        va = jnp.concatenate([x0, x2[0:56]], axis=0)
        vb = jnp.concatenate([x1, x2[64:120]], axis=0)
        early = jnp.where(first_half, va, pltpu.roll(vb, 64, 1))
        late = jnp.where(first_half, pltpu.roll(va, 64, 1), vb)
        return early, late

    def total(x):
        return jnp.sum(x, axis=(0, 1), keepdims=True)

    zero8 = jnp.zeros((8, 128), F32)

    g0[...] = back(0)
    forward(0, g0[...])

    def rays0(p, acc):
        x = rays(p)
        q0[p] = x
        z_of(p, x)
        return acc + squares(x)

    norm_q0 = lax.fori_loop(0, PAIRS, rays0, zero8)
    ar_put(0, 0, jnp.concatenate([squares(g0[...]), norm_q0], axis=0))
    h0 = back(
        1,
        (
            lambda: ar_put(0, 1, ar_get(0, 0)),
            lambda: ar_put(0, 2, ar_get(0, 1)),
        ),
    )
    sums = ar_get(0, 2)
    gamma0 = total(sums[0:8])
    alpha0 = gamma0 / total(sums[8:16])
    g1[...] = g0[...] - alpha0 * h0
    ar_put(1, 0, jnp.concatenate([squares(g1[...]), zero8], axis=0))

    def first_residual(p, _):
        early, late = to_columns(q0[p])
        for base, x in ((0, early), (512, late)):
            at = pl.ds(pl.multiple_of(base + p * 128, 128), 128)
            r1[:, at] = meas_ref[:, at] - alpha0 * x
        return 0

    forward(
        1,
        g1[...],
        (
            lambda: ar_put(1, 1, ar_get(1, 0)),
            lambda: ar_put(1, 2, ar_get(1, 1)),
            lambda: lax.fori_loop(0, PAIRS, first_residual, 0),
        ),
    )
    sums = ar_get(1, 2)
    gamma1 = total(sums[0:8])
    beta = gamma1 / gamma0
    d1[...] = g1[...] + beta * g0[...]

    def rays1(p, acc):
        x = rays(p) + beta * q0[p]
        q1[p] = x
        z_of(p, x)
        return acc + squares(x)

    norm_q1 = lax.fori_loop(0, PAIRS, rays1, zero8)
    ar_put(2, 0, jnp.concatenate([norm_q1, zero8], axis=0))
    h1 = back(
        2,
        (
            lambda: ar_put(2, 1, ar_get(2, 0)),
            lambda: ar_put(2, 2, ar_get(2, 1)),
        ),
    )
    sums = ar_get(2, 2)
    alpha1 = gamma1 / total(sums[0:8])
    grad_ref[...] = g1[...] - alpha1 * h1
    vol_ref[...] = alpha0 * g0[...] + alpha1 * d1[...]

    def last_residual(p, _):
        early, late = to_columns(q1[p])
        for base, x in ((0, early), (512, late)):
            at = pl.ds(pl.multiple_of(base + p * 128, 128), 128)
            res_ref[:, at] = r1[:, at] - alpha1 * x
        return 0

    lax.fori_loop(0, PAIRS, last_residual, 0)

    for phase in range(3):
        for i in range(NCOL):
            for side in range(2):
                b_rim(phase, i, side).wait_send()
        for h in range(2):
            b_relay(phase, h).wait_send()
            for side in range(2):
                b_direct(phase, side, h).wait_send()
    for phase in range(2):
        for h in range(2):
            a_forward(phase, h).wait_send()
            for side in range(2):
                a_main(phase, side, h).wait_send()
            for i in range(NCOL):
                a_rim(phase, i, h).wait_send()


def on_device(lo_size, measured, view_offset, tile_index, footprint, transaxial):
    hi_size = lax.axis_size("gz") // lo_size
    n_ar = NCOL + lo_size + hi_size
    vmem = pl.BlockSpec(memory_space=pltpu.VMEM)
    smem = pl.BlockSpec(memory_space=pltpu.SMEM)
    dma = pltpu.SemaphoreType.DMA
    scratch = [
        pltpu.VMEM((NA, C, NXW), F32),
        pltpu.VMEM((NCOL, KC, VX), BF16),
        pltpu.VMEM((NCOL, KC, VX), BF16),
        pltpu.VMEM((128, 128), F32),
        pltpu.VMEM((TOP + WZ, 128), F32),
        pltpu.VMEM((NA, WZ, 128), BF16),
        pltpu.VMEM((NA, WZ, 128), BF16),
        pltpu.VMEM((NA, 128, WZ), BF16),
        pltpu.VMEM((NA, 128, WZ), BF16),
        pltpu.VMEM((WZ, KC), BF16),
        pltpu.VMEM((WZ, KC), BF16),
        pltpu.VMEM((ZS, KC), F32),
        pltpu.VMEM((ZS, KC), F32),
        pltpu.VMEM((PAIRS, 128, PW), F32),
        pltpu.VMEM((PAIRS, 128, PW), F32),
        pltpu.VMEM((C, 2 * NA * R), F32),
        pltpu.VMEM((3, NCOL, WZ, VX), F32),
        pltpu.VMEM((3, NCOL, HR, VX), F32),
        pltpu.VMEM((3, NCOL, HR, VX), F32),
        pltpu.VMEM((3, 2, 64, VX), F32),
        pltpu.VMEM((3, 2, 2, 64, VX), F32),
        pltpu.VMEM((2, NCOL, WZ, VX), F32),
        pltpu.VMEM((ZS, VX), F32),
        pltpu.VMEM((ZS, VX), F32),
        pltpu.VMEM((ZS, VX), F32),
        pltpu.VMEM((3, NCOL, 16, 128), F32),
        pltpu.VMEM((3, lo_size, 16, 128), F32),
        pltpu.VMEM((3, hi_size, 16, 128), F32),
        dma((NA,)),
        dma((3, 14)),
        dma((3, 14)),
        dma((2, 14)),
        dma((2, 14)),
        dma((3, n_ar)),
        dma((3, n_ar)),
    ]
    return pl.pallas_call(
        functools.partial(kernel, lo_size),
        out_shape=(
            jax.ShapeDtypeStruct((ZS, VX), F32),
            jax.ShapeDtypeStruct((C, 2 * NA * R), F32),
            jax.ShapeDtypeStruct((ZS, VX), F32),
        ),
        in_specs=[smem, smem, vmem, vmem, pl.BlockSpec(memory_space=pl.ANY)],
        out_specs=(vmem, vmem, vmem),
        scratch_shapes=scratch,
        compiler_params=pltpu.CompilerParams(
            collective_id=0, has_side_effects=True, vmem_limit_bytes=56 * 1024 * 1024
        ),
        cost_estimate=pl.CostEstimate(flops=12_000_000_000, bytes_accessed=9_000_000, transcendentals=0),
    )(view_offset, tile_index, footprint, measured, transaxial)


def solution(mesh):
    lo_size = min(8, mesh.shape["gz"] // 2)
    return jax.shard_map(
        functools.partial(on_device, lo_size),
        mesh=mesh,
        in_specs=(P("col", "gz"), P("gz"), P("gz"), P(), P(None, "col", None)),
        out_specs=(P("gz", "col"), P("col", "gz"), P("gz", "col")),
        check_vma=False,
    )
```

```python
import functools

import jax
import jax.numpy as jnp
from jax import lax
from jax.experimental import pallas as pl
from jax.experimental.pallas import tpu as pltpu
from jax.sharding import PartitionSpec as P

MESH = pl.DeviceIdType.MESH
F32 = jnp.float32
BF16 = jnp.bfloat16

NA = 8
R = 64
ZW = 32
ZS = 128
HR = 64
WZ = 256
C = 184
NXW = 1024
NCOL = 4
VX = NXW // NCOL
PAIRS = NA // 2
PW = 384
KC = PAIRS * PW
TOP = WZ - ZW
CHUNK = 512
NT = (((1,), (1,)), ((), ()))
NN = (((1,), (0,)), ((), ()))


def split(x):
    hi = x.astype(BF16)
    return hi, (x - hi.astype(F32)).astype(BF16)


def dot(a, b, dims):
    return lax.dot_general(a, b, dimension_numbers=dims, preferred_element_type=F32)


def dot3(a_hi, a_lo, b_hi, b_lo, dims):
    return dot(a_hi, b_hi, dims) + (dot(a_lo, b_hi, dims) + dot(a_hi, b_lo, dims))


def squares(x):
    rows, lanes = x.shape
    y = jnp.sum((x * x).reshape(rows // 8, 8, lanes), axis=0)
    return sum(y[:, k * 128 : (k + 1) * 128] for k in range(lanes // 128))


def total(x):
    return jnp.sum(x, axis=(0, 1), keepdims=True)


def kernel(
    lo_size,
    off_ref, tile_ref, foot_ref, meas_ref, trans_ref,
    vol_ref, res_ref, grad_ref,
    stage, t_hi, t_lo, shifted, w_hi, w_lo,
    z_both, q_all, q0, q1, r1,
    part, rim, direct,
    window, g0, g1, h0, l0,
    ar1, ar2,
    t_sem, rim_send, rim_recv, dir_send, dir_recv,
    gat_send, gat_recv, win_send, win_recv, ar_send, ar_recv,
):
    n_gz = lax.axis_size("gz")
    hi_size = n_gz // lo_size
    x_size = lo_size // 2
    gz = lax.axis_index("gz")
    y = lax.axis_index("col")
    z_at = lax.div(gz, lo_size)
    x_at = lax.div(lax.rem(gz, lo_size), 2)
    core = lax.rem(gz, 2)
    inner, outer = 1 - core, core

    def col(d):
        return lax.rem(y + d, NCOL)

    def flat_peer(d):
        at = lax.rem(x_at * NCOL + y + d, x_size * NCOL)
        return (z_at * lo_size + lax.div(at, NCOL) * 2 + core, lax.rem(at, NCOL))

    def deep_peer(d):
        at = lax.rem(z_at * 2 + core + d, hi_size * 2)
        return (lax.div(at, 2) * lo_size + x_at * 2 + lax.rem(at, 2), y)

    groups = ((x_size * NCOL, flat_peer), (hi_size * 2, deep_peer))

    barrier = pltpu.get_barrier_semaphore()

    def greet(to):
        pl.semaphore_signal(barrier, inc=1, device_id=to, device_id_type=MESH)

    for size, peer in groups:
        lax.fori_loop(1, size, lambda d, c, peer=peer: (greet(peer(d)), c)[1], 0)
    for other in (1, n_gz - 1):
        greet((lax.rem(gz + other, n_gz), y))
        greet((lax.rem(gz + other, n_gz), col(2)))
    greeted = groups[0][0] + groups[1][0] + 2

    loads = [pltpu.make_async_copy(trans_ref.at[a], stage.at[a], t_sem.at[a]) for a in range(NA)]
    for load in loads:
        load.start()

    lane = lax.broadcasted_iota(jnp.int32, (1, 128), 1)
    first_half = lane < 64

    shifted[...] = jnp.zeros_like(shifted)

    def place(a, _):
        shifted[TOP:WZ, :] = jnp.concatenate(
            [foot_ref[tile_ref[a]], foot_ref[tile_ref[a + NA]]], axis=1
        )
        one = shifted[pl.ds(TOP - off_ref[a], WZ), :]
        two = shifted[pl.ds(TOP - off_ref[a + NA], WZ), :]
        hi, lo = split(jnp.where(first_half, one, two))
        w_hi[a] = hi
        w_lo[a] = lo
        return 0

    lax.fori_loop(0, NA, place, 0)

    def z_of(p, x):
        hi, lo = split(x)
        pick = lambda v, k: jnp.concatenate([v[k * 128 : (k + 1) * 128], v[256:]], axis=0)
        za = dot3(w_hi[2 * p], w_lo[2 * p], pick(hi, 0), pick(lo, 0), NT)
        zb = dot3(w_hi[2 * p + 1], w_lo[2 * p + 1], pick(hi, 1), pick(lo, 1), NT)
        third = jnp.where(first_half, za[:, 128:], zb[:, 128:])
        hi, lo = split(jnp.concatenate([za[:, :128], zb[:, :128], third], axis=1))
        at = pl.ds(pl.multiple_of(p * PW, 128), PW)
        z_both[0:WZ, at] = hi
        z_both[WZ:, at] = lo

    def early_at(p):
        return pl.ds(pl.multiple_of(p * 128, 128), 128)

    def late_at(p):
        return pl.ds(pl.multiple_of(NA * R + p * 128, 128), 128)

    def z_of_measured(p, _):
        early = meas_ref[:, early_at(p)]
        late = meas_ref[:, late_at(p)]
        a = jnp.where(first_half, early, pltpu.roll(late, 64, 1))
        b = jnp.where(first_half, pltpu.roll(early, 64, 1), late)
        gap = jnp.zeros((8, 128), F32)
        z_of(p, jnp.concatenate([a[:128], b[:128], a[128:], gap, b[128:], gap], axis=0))
        return 0

    def as_measured(x):
        a = jnp.concatenate([x[0:128], x[256:312]], axis=0)
        b = jnp.concatenate([x[128:256], x[320:376]], axis=0)
        early = jnp.where(first_half, a, pltpu.roll(b, 64, 1))
        late = jnp.where(first_half, pltpu.roll(a, 64, 1), b)
        return early, late

    lax.fori_loop(0, PAIRS, z_of_measured, 0)

    def convert(p, _):
        for h in range(2):
            a = 2 * p + h
            pltpu.make_async_copy(trans_ref.at[a], stage.at[a], t_sem.at[a]).wait()
        base = p * PW
        for s in range(NCOL):
            cols = slice(s * VX, (s + 1) * VX)
            for h in range(2):
                a = 2 * p + h
                hi, lo = split(stage[a, 0:128, cols])
                at = pl.ds(pl.multiple_of(base + h * 128, 64), 128)
                t_hi[s, at] = hi
                t_lo[s, at] = lo
                tail = jnp.concatenate([stage[a, 128:C, cols], jnp.zeros((8, VX), F32)], axis=0)
                hi, lo = split(tail)
                at = pl.ds(pl.multiple_of(base + 256 + h * 64, 64), 64)
                t_hi[s, at] = hi
                t_lo[s, at] = lo
        return 0

    lax.fori_loop(0, PAIRS, convert, 0)

    pl.semaphore_wait(barrier, greeted)

    def remote(src, dst, send, recv, to):
        return pltpu.make_async_remote_copy(
            src_ref=src, dst_ref=dst, send_sem=send, recv_sem=recv, device_id=to, device_id_type=MESH
        )

    ar_bufs = (ar1, ar2)
    ar_at = (x_at * NCOL + y, z_at * 2 + core)
    ar_base = (0, x_size * NCOL)

    def ar_copy(k, level, d):
        slot = ar_bufs[level].at[k, ar_at[level]]
        sem = ar_base[level] + d
        return remote(slot, slot, ar_send.at[k, sem], ar_recv.at[k, sem], groups[level][1](d))

    def ar_put(k, level, value):
        ar_bufs[level][k, ar_at[level]] = value

        def go(d, _):
            ar_copy(k, level, d).start()
            return 0

        lax.fori_loop(1, groups[level][0], go, 0)

    def ar_get(k, level):
        def done(d, _):
            ar_copy(k, level, d).wait()
            return 0

        lax.fori_loop(1, groups[level][0], done, 0)
        return jnp.sum(ar_bufs[level][k], axis=0)

    def ar_first(k, one, two):
        rows = [jnp.sum(v, axis=0, keepdims=True) for v in (one, two)]
        ar_put(k, 0, jnp.concatenate(rows, axis=0))

    def ar_second(k):
        ar_put(k, 1, ar_get(k, 0))

    def half(h, base=HR):
        return pl.ds(pl.multiple_of(base + h * 64, 64), 64)

    def edge(h):
        return pl.ds(pl.multiple_of((1 - h) * (WZ - HR), 64), HR)

    def b_rim(phase, i, h):
        return remote(
            part.at[phase, i, edge(h)], rim.at[phase, i, h],
            rim_send.at[phase, i, h], rim_recv.at[phase, i, h],
            (lax.rem(gz + n_gz + 1 - 2 * h, n_gz), y),
        )

    def owner(i):
        return lax.rem(y + 2 + 3 * i + 3 * lax.div(i * (i - 1), 2), NCOL)

    def b_direct(phase, i, h):
        return remote(
            part.at[phase, i, half(h)], direct.at[phase, i, half(h, 0)],
            dir_send.at[phase, i, h], dir_recv.at[phase, i, h], (gz, owner(i)),
        )

    def with_rim(phase, i, h):
        b_rim(phase, i, h).wait_recv()
        inside = jnp.where(h == 0, gz > 0, gz < n_gz - 1)
        return part[phase, i, half(h)] + jnp.where(inside, rim[phase, i, h], 0.0)

    def send_half(phase, i, h):
        part[phase, i, half(h)] = with_rim(phase, i, h)
        b_direct(phase, i, h).start()

    def back(phase, take, beside0=None, beside1=None, beside2=None):
        def product(i, _):
            s = owner(i)
            both = dot(z_both[...], t_hi[s], NN)
            part[phase, i] = both[0:WZ] + (both[WZ:] + dot(z_both[0:WZ], t_lo[s], NN))
            b_rim(phase, i, inner).start()
            b_rim(phase, i, outer).start()

            @pl.when(i > 0)
            def _():
                send_half(phase, i - 1, inner)

            if beside0 is not None:

                @pl.when(i == 0)
                def _():
                    beside0()

            return 0

        lax.fori_loop(0, NCOL, product, 0)
        send_half(phase, 0, outer)
        if beside1 is not None:
            beside1()
        send_half(phase, 1, outer)
        send_half(phase, 2, outer)
        if beside2 is not None:
            beside2()
        for h, far in ((inner, False), (outer, True)):
            own = with_rim(phase, 3, h)
            for i in range(3):
                b_direct(phase, i, h).wait_recv()
            d = [direct[phase, i, half(h, 0)] for i in range(3)]
            take(h, own + (d[0] + (d[1] + d[2])), far)

    def a_main(phase, i, h):
        return remote(
            window.at[phase, 0, half(h)], window.at[phase, i, half(h)],
            gat_send.at[phase, i, h], gat_recv.at[phase, i, h],
            (gz, lax.rem(y + i + lax.div(i, 2) + 2 * lax.div(i, 3), NCOL)),
        )

    def a_rim(phase, i, h, far=False):
        src = window.at[phase, 0 if far else i, half(h)]
        return remote(
            src, window.at[phase, i, edge(h)],
            win_send.at[phase, i, h], win_recv.at[phase, i, h],
            (lax.rem(gz + n_gz - 1 + 2 * h, n_gz), col(2) if far else y),
        )

    def gather_start(phase, h, far):
        for i in (3, 1, 2):
            a_main(phase, i, h).start()
        a_rim(phase, 0, h).start()
        if far:
            a_rim(phase, 3, h, True).start()

    def gather_product(phase, i):
        s = lax.rem(y + 3 * i + 3 * ((i * (i - 1)) // 2), NCOL)
        low = jnp.where(gz > 0, window[phase, i, 0:HR], 0.0)
        high = jnp.where(gz < n_gz - 1, window[phase, i, WZ - HR : WZ], 0.0)
        hi, lo = split(jnp.concatenate([low, window[phase, i, HR : HR + ZS], high], axis=0))

        def some(n, _):
            at = pl.ds(pl.multiple_of(n * CHUNK, CHUNK), CHUNK)
            value = dot3(t_hi[s, at], t_lo[s, at], hi, lo, NT)
            if i == 0:
                q_all[at] = value
            else:
                q_all[at] += value
            return 0

        lax.fori_loop(0, KC // CHUNK, some, 0)

    def gather(phase, beside0=None, beside1=None):
        def wait_rims(i):
            for h in range(2):
                a_rim(phase, i, h).wait_recv()

        if beside0 is not None:
            beside0()
        for h in (inner, outer):
            for i in (1, 2):
                a_main(phase, i, h).wait_recv()
                a_rim(phase, i, h).start()
        wait_rims(0)
        gather_product(phase, 0)
        if beside1 is not None:
            beside1()
        for h in (inner, outer):
            a_main(phase, 3, h).wait_recv()
        a_rim(phase, 3, inner).start()
        for i in (1, 2, 3):
            wait_rims(i)
            gather_product(phase, i)

    def rays(p):
        hi, lo = split(q_all[pl.ds(pl.multiple_of(p * PW, 128), PW)])

        def one(a, k):
            pick = lambda v: jnp.concatenate(
                [v[k * 128 : (k + 1) * 128], v[256 + k * 64 : 320 + k * 64]], axis=0
            )
            return dot3(pick(hi), pick(lo), w_hi[a], w_lo[a], NN)

        pa = one(2 * p, 0)
        pb = one(2 * p + 1, 1)
        return jnp.concatenate([pa[:128], pb[:128], pa[128:], pb[128:]], axis=0)

    zero8 = jnp.zeros((8, 128), F32)

    def take_g0(h, value, far):
        g0[half(h, 0)] = value
        window[0, 0, half(h)] = value
        gather_start(0, h, far)

    back(0, take_g0)
    gather(0)

    def rays0(p, acc):
        x = rays(p)
        q0[p] = x
        z_of(p, x)
        return acc + squares(x)

    norm_q0 = lax.fori_loop(0, PAIRS, rays0, zero8)
    ar_first(0, squares(g0[...]), norm_q0)

    def take_h0(h, value, _):
        h0[half(h, 0)] = value

    back(1, take_h0, beside1=lambda: ar_second(0))
    sums = ar_get(0, 1)
    gamma0 = total(sums[0:1])
    alpha0 = gamma0 / total(sums[1:2])
    for h, far in ((outer, True), (inner, False)):
        value = g0[half(h, 0)] - alpha0 * h0[half(h, 0)]
        g1[half(h, 0)] = value
        window[1, 0, half(h)] = value
        gather_start(1, h, far)
    ar_first(1, squares(g1[...]), zero8)

    def first_residual(p, _):
        early, late = as_measured(q0[p])
        r1[:, early_at(p)] = meas_ref[:, early_at(p)] - alpha0 * early
        r1[:, late_at(p)] = meas_ref[:, late_at(p)] - alpha0 * late
        return 0

    gather(1, lambda: lax.fori_loop(0, PAIRS, first_residual, 0), lambda: ar_second(1))

    def rays1(p, _):
        x = rays(p)
        q1[p] = x
        z_of(p, x)
        return 0

    lax.fori_loop(0, PAIRS, rays1, 0)

    gamma1 = total(ar_get(1, 1)[0:1])
    beta = gamma1 / gamma0

    def rays2(p, acc):
        x = q1[p] + beta * q0[p]
        q1[p] = x
        return acc + squares(x)

    ar_first(2, lax.fori_loop(0, PAIRS, rays2, zero8), zero8)

    def take_l0(h, value, _):
        l0[half(h, 0)] = value

    def image_out():
        def some(p, _):
            early, late = as_measured(q1[p])
            res_ref[:, early_at(p)] = early
            res_ref[:, late_at(p)] = late
            return 0

        lax.fori_loop(0, PAIRS, some, 0)

    back(2, take_l0, beside1=lambda: ar_second(2), beside2=image_out)
    sums = ar_get(2, 1)
    alpha1 = gamma1 / total(sums[0:1])
    grad_ref[...] = g1[...] - alpha1 * (l0[...] + beta * h0[...])
    vol_ref[...] = alpha0 * g0[...] + alpha1 * (g1[...] + beta * g0[...])
    res_ref[...] = r1[...] - alpha1 * res_ref[...]

    for phase in range(3):
        for h in range(2):
            for i in range(NCOL):
                b_rim(phase, i, h).wait_send()
            for i in range(3):
                b_direct(phase, i, h).wait_send()
    for phase in range(2):
        for h in range(2):
            for i in range(NCOL):
                a_rim(phase, i, h).wait_send()
            for i in range(1, NCOL):
                a_main(phase, i, h).wait_send()


def hand_on(a_ref, b_ref, c_ref, x_ref, y_ref, z_ref, sem):
    copies = [
        pltpu.make_async_copy(s, d, sem.at[k])
        for k, (s, d) in enumerate(((a_ref, x_ref), (b_ref, y_ref), (c_ref, z_ref)))
    ]
    for copy in copies:
        copy.start()
    for copy in copies:
        copy.wait()


def on_device(lo_size, measured, view_offset, tile_index, footprint, transaxial):
    hi_size = lax.axis_size("gz") // lo_size
    flat, deep = lo_size // 2 * NCOL, hi_size * 2
    vmem = pl.BlockSpec(memory_space=pltpu.VMEM)
    smem = pl.BlockSpec(memory_space=pltpu.SMEM)
    hbm = pl.BlockSpec(memory_space=pltpu.HBM)
    dma = pltpu.SemaphoreType.DMA
    scratch = [
        pltpu.VMEM((NA, C, NXW), F32),
        pltpu.VMEM((NCOL, KC, VX), BF16),
        pltpu.VMEM((NCOL, KC, VX), BF16),
        pltpu.VMEM((TOP + WZ, 128), F32),
        pltpu.VMEM((NA, WZ, 128), BF16),
        pltpu.VMEM((NA, WZ, 128), BF16),
        pltpu.VMEM((2 * WZ, KC), BF16),
        pltpu.VMEM((KC, WZ), F32),
        pltpu.VMEM((PAIRS, PW, 128), F32),
        pltpu.VMEM((PAIRS, PW, 128), F32),
        pltpu.VMEM((C, 2 * NA * R), F32),
        pltpu.VMEM((3, NCOL, WZ, VX), F32),
        pltpu.VMEM((3, NCOL, 2, HR, VX), F32),
        pltpu.VMEM((3, 3, ZS, VX), F32),
        pltpu.VMEM((2, NCOL, WZ, VX), F32),
        pltpu.VMEM((ZS, VX), F32),
        pltpu.VMEM((ZS, VX), F32),
        pltpu.VMEM((ZS, VX), F32),
        pltpu.VMEM((ZS, VX), F32),
        pltpu.VMEM((3, flat, 2, 128), F32),
        pltpu.VMEM((3, deep, 2, 128), F32),
        dma((NA,)),
        dma((3, NCOL, 2)),
        dma((3, NCOL, 2)),
        dma((3, 3, 2)),
        dma((3, 3, 2)),
        dma((2, NCOL, 2)),
        dma((2, NCOL, 2)),
        dma((2, NCOL, 2)),
        dma((2, NCOL, 2)),
        dma((3, flat + deep)),
        dma((3, flat + deep)),
    ]
    shapes = (
        jax.ShapeDtypeStruct((ZS, VX), F32),
        jax.ShapeDtypeStruct((C, 2 * NA * R), F32),
        jax.ShapeDtypeStruct((ZS, VX), F32),
    )
    outs = pl.pallas_call(
        functools.partial(kernel, lo_size),
        out_shape=shapes,
        in_specs=[smem, smem, vmem, vmem, pl.BlockSpec(memory_space=pl.ANY)],
        out_specs=(vmem, vmem, vmem),
        scratch_shapes=scratch,
        compiler_params=pltpu.CompilerParams(
            collective_id=0, has_side_effects=True, vmem_limit_bytes=56 * 1024 * 1024
        ),
        cost_estimate=pl.CostEstimate(flops=12_000_000_000, bytes_accessed=9_000_000, transcendentals=0),
    )(view_offset, tile_index, jnp.swapaxes(footprint, 1, 2), measured, transaxial)
    return pl.pallas_call(
        hand_on,
        out_shape=shapes,
        in_specs=[hbm] * 3,
        out_specs=(hbm,) * 3,
        scratch_shapes=[dma((3,))],
        compiler_params=pltpu.CompilerParams(vmem_limit_bytes=60 * 1024 * 1024),
    )(*outs)


def solution(mesh):
    lo_size = min(8, mesh.shape["gz"] // 2)
    return jax.shard_map(
        functools.partial(on_device, lo_size),
        mesh=mesh,
        in_specs=(P("col", "gz"), P("gz"), P("gz"), P(), P(None, "col", None)),
        out_specs=(P("gz", "col"), P("col", "gz"), P("gz", "col")),
        check_vma=False,
    )
```

```python
import functools

import jax
import jax.numpy as jnp
from jax import lax
from jax.experimental import pallas as pl
from jax.experimental.pallas import tpu as pltpu
from jax.sharding import PartitionSpec as P

MESH = pl.DeviceIdType.MESH
F32 = jnp.float32
BF16 = jnp.bfloat16

NA = 8
R = 64
ZW = 32
ZS = 128
HR = 64
WZ = 256
C = 184
NXW = 1024
NCOL = 4
VX = NXW // NCOL
PAIRS = NA // 2
PW = 384
KC = PAIRS * PW
TOP = WZ - ZW
SCALE = 2.0**40
NT = (((1,), (1,)), ((), ()))
NN = (((1,), (0,)), ((), ()))


def split(x):
    hi = x.astype(BF16)
    return hi, (x - hi.astype(F32)).astype(BF16)


def dot(a, b, dims):
    return lax.dot_general(a, b, dimension_numbers=dims, preferred_element_type=F32)


def dot3(a_hi, a_lo, b_hi, b_lo, dims):
    a = jnp.concatenate([a_hi, a_lo, a_hi], axis=dims[0][0][0])
    b = jnp.concatenate([b_hi, b_hi, b_lo], axis=dims[0][1][0])
    return dot(a, b, dims)


def squares(x):
    rows, lanes = x.shape
    y = jnp.sum((x * x).reshape(rows // 8, 8, lanes), axis=0)
    return sum(y[:, k * 128 : (k + 1) * 128] for k in range(lanes // 128))


def total(x):
    return jnp.sum(x, axis=(0, 1), keepdims=True)


def kernel(
    lo_size,
    off_ref, tile_ref, foot_ref, measured_ref, trans_ref,
    vol_ref, res_ref, grad_ref,
    stage, t_hi, t_lo, shifted, w_hi, w_lo,
    z_both, q_all, q0, q1, r1,
    part, rim, direct,
    window, g0, g1, h0, l0, scalars,
    ar1, ar2,
    meas_ref, m_sem, t_sem, rim_send, rim_recv, dir_send, dir_recv,
    gat_send, gat_recv, win_send, win_recv, ar_send, ar_recv,
):
    n_gz = lax.axis_size("gz")
    hi_size = n_gz // lo_size
    x_size = lo_size // 2
    gz = lax.axis_index("gz")
    y = lax.axis_index("col")
    z_at = lax.div(gz, lo_size)
    x_at = lax.div(lax.rem(gz, lo_size), 2)
    core = lax.rem(gz, 2)
    inner, outer = 1 - core, core

    def col(d):
        return lax.rem(y + d, NCOL)

    def flat_peer(d):
        at = lax.rem(x_at * NCOL + y + d, x_size * NCOL)
        return (z_at * lo_size + lax.div(at, NCOL) * 2 + core, lax.rem(at, NCOL))

    def deep_peer(d):
        at = lax.rem(z_at * 2 + core + d, hi_size * 2)
        return (lax.div(at, 2) * lo_size + x_at * 2 + lax.rem(at, 2), y)

    groups = ((x_size * NCOL, flat_peer), (hi_size * 2, deep_peer))

    barrier = pltpu.get_barrier_semaphore()

    def greet(to):
        pl.semaphore_signal(barrier, inc=1, device_id=to, device_id_type=MESH)

    for size, peer in groups:
        lax.fori_loop(1, size, lambda d, c, peer=peer: (greet(peer(d)), c)[1], 0)
    for other in (1, n_gz - 1):
        greet((lax.rem(gz + other, n_gz), y))
        greet((lax.rem(gz + other, n_gz), col(2)))
    greeted = groups[0][0] + groups[1][0] + 2

    loads = [pltpu.make_async_copy(trans_ref.at[a], stage.at[a], t_sem.at[a]) for a in range(NA)]
    meas_load = pltpu.make_async_copy(measured_ref, meas_ref, m_sem)
    meas_load.start()
    for load in loads:
        load.start()

    lane = lax.broadcasted_iota(jnp.int32, (1, 128), 1)
    first_half = lane < 64

    shifted[...] = jnp.zeros_like(shifted)

    def place(a, _):
        shifted[TOP:WZ, :] = jnp.concatenate(
            [foot_ref[tile_ref[a]], foot_ref[tile_ref[a + NA]]], axis=1
        )
        one = shifted[pl.ds(TOP - off_ref[a], WZ), :]
        two = shifted[pl.ds(TOP - off_ref[a + NA], WZ), :]
        hi, lo = split(jnp.where(first_half, one, two))
        w_hi[a] = hi
        w_lo[a] = lo
        return 0

    lax.fori_loop(0, NA, place, 0)

    def z_of(p, x):
        hi, lo = split(x)
        pick = lambda v, k: jnp.concatenate([v[k * 128 : (k + 1) * 128], v[256:]], axis=0)
        za = dot3(w_hi[2 * p], w_lo[2 * p], pick(hi, 0), pick(lo, 0), NT)
        zb = dot3(w_hi[2 * p + 1], w_lo[2 * p + 1], pick(hi, 1), pick(lo, 1), NT)
        third = jnp.where(first_half, za[:, 128:], zb[:, 128:])
        hi, lo = split(jnp.concatenate([za[:, :128], zb[:, :128], third], axis=1))
        at = pl.ds(pl.multiple_of(p * PW, 128), PW)
        z_both[0:WZ, at] = hi
        z_both[WZ:, at] = lo

    def early_at(p):
        return pl.ds(pl.multiple_of(p * 128, 128), 128)

    def late_at(p):
        return pl.ds(pl.multiple_of(NA * R + p * 128, 128), 128)

    def z_of_measured(p, _):
        early = meas_ref[:, early_at(p)]
        late = meas_ref[:, late_at(p)]
        a = jnp.where(first_half, early, pltpu.roll(late, 64, 1))
        b = jnp.where(first_half, pltpu.roll(early, 64, 1), late)
        gap = jnp.zeros((8, 128), F32)
        z_of(p, jnp.concatenate([a[:128], b[:128], a[128:], gap, b[128:], gap], axis=0))
        return 0

    def as_measured(x):
        a = jnp.concatenate([x[0:128], x[256:312]], axis=0)
        b = jnp.concatenate([x[128:256], x[320:376]], axis=0)
        early = jnp.where(first_half, a, pltpu.roll(b, 64, 1))
        late = jnp.where(first_half, pltpu.roll(a, 64, 1), b)
        return early, late

    meas_load.wait()
    lax.fori_loop(0, PAIRS, z_of_measured, 0)

    def convert(p, _):
        for h in range(2):
            a = 2 * p + h
            pltpu.make_async_copy(trans_ref.at[a], stage.at[a], t_sem.at[a]).wait()
        base = p * PW
        for s in range(NCOL):
            cols = slice(s * VX, (s + 1) * VX)
            for h in range(2):
                a = 2 * p + h
                hi, lo = split(stage[a, 0:128, cols])
                at = pl.ds(pl.multiple_of(base + h * 128, 64), 128)
                t_hi[s, at] = hi
                t_lo[s, at] = lo
                tail = jnp.concatenate([stage[a, 128:C, cols], jnp.zeros((8, VX), F32)], axis=0)
                hi, lo = split(tail)
                at = pl.ds(pl.multiple_of(base + 256 + h * 64, 64), 64)
                t_hi[s, at] = hi
                t_lo[s, at] = lo
        return 0

    lax.fori_loop(0, PAIRS, convert, 0)

    pl.semaphore_wait(barrier, greeted)

    def remote(src, dst, send, recv, to):
        return pltpu.make_async_remote_copy(
            src_ref=src, dst_ref=dst, send_sem=send, recv_sem=recv, device_id=to, device_id_type=MESH
        )

    ar_bufs = (ar1, ar2)
    ar_at = (x_at * NCOL + y, z_at * 2 + core)
    ar_base = (0, x_size * NCOL)

    def ar_copy(k, level, d):
        slot = ar_bufs[level].at[k, ar_at[level]]
        sem = ar_base[level] + d
        return remote(slot, slot, ar_send.at[k, sem], ar_recv.at[k, sem], groups[level][1](d))

    def ar_put(k, level, value):
        ar_bufs[level][k, ar_at[level]] = value

        def go(d, _):
            ar_copy(k, level, d).start()
            return 0

        lax.fori_loop(1, groups[level][0], go, 0)

    def ar_get(k, level):
        def done(d, _):
            ar_copy(k, level, d).wait()
            return 0

        lax.fori_loop(1, groups[level][0], done, 0)
        return jnp.sum(ar_bufs[level][k], axis=0)

    def ar_first(k, one, two):
        rows = [jnp.sum(v, axis=0, keepdims=True) for v in (one, two)]
        ar_put(k, 0, jnp.concatenate(rows, axis=0))

    def ar_second(k):
        ar_put(k, 1, ar_get(k, 0))

    def half(h, base=HR):
        return pl.ds(pl.multiple_of(base + h * 64, 64), 64)

    def edge(h):
        return pl.ds(pl.multiple_of((1 - h) * (WZ - HR), 64), HR)

    def b_rim(phase, i, h):
        return remote(
            part.at[phase, i, edge(h)], rim.at[phase, i, h],
            rim_send.at[phase, i, h], rim_recv.at[phase, i, h],
            (lax.rem(gz + n_gz + 1 - 2 * h, n_gz), y),
        )

    def owner(i):
        return lax.rem(y + 2 + 3 * i + 3 * lax.div(i * (i - 1), 2), NCOL)

    def b_direct(phase, i, h):
        return remote(
            part.at[phase, i, half(h)], direct.at[phase, i, half(h, 0)],
            dir_send.at[phase, i, h], dir_recv.at[phase, i, h], (gz, owner(i)),
        )

    def with_rim(phase, i, h):
        b_rim(phase, i, h).wait_recv()
        inside = jnp.where(h == 0, gz > 0, gz < n_gz - 1)
        return part[phase, i, half(h)] + jnp.where(inside, rim[phase, i, h], 0.0)

    def send_half(phase, i, h):
        part[phase, i, half(h)] = with_rim(phase, i, h)
        b_direct(phase, i, h).start()

    def back(phase, take, beside1=None, beside2=None):
        def product(i, _):
            s = owner(i)
            both = dot(z_both[...], t_hi[s], NN)
            part[phase, i] = both[0:WZ] + (both[WZ:] + dot(z_both[0:WZ], t_lo[s], NN))
            b_rim(phase, i, inner).start()
            b_rim(phase, i, outer).start()

            @pl.when(i > 0)
            def _():
                send_half(phase, i - 1, inner)

            return 0

        lax.fori_loop(0, NCOL, product, 0)
        send_half(phase, 0, outer)
        send_half(phase, 1, outer)
        if beside1 is not None:
            beside1()
        send_half(phase, 2, outer)
        if beside2 is not None:
            beside2()
        for h, far in ((inner, False), (outer, True)):
            own = with_rim(phase, 3, h)
            for i in range(3):
                b_direct(phase, i, h).wait_recv()
            d = [direct[phase, i, half(h, 0)] for i in range(3)]
            take(h, own + (d[0] + (d[1] + d[2])), far)

    def a_main(phase, i, h):
        return remote(
            window.at[phase, 0, half(h)], window.at[phase, i, half(h)],
            gat_send.at[phase, i, h], gat_recv.at[phase, i, h],
            (gz, lax.rem(y + i + lax.div(i, 2) + 2 * lax.div(i, 3), NCOL)),
        )

    def a_rim(phase, i, h, far=False):
        src = window.at[phase, 0 if far else i, half(h)]
        return remote(
            src, window.at[phase, i, edge(h)],
            win_send.at[phase, i, h], win_recv.at[phase, i, h],
            (lax.rem(gz + n_gz - 1 + 2 * h, n_gz), col(2) if far else y),
        )

    def gather_start(phase, h, far):
        a_rim(phase, 0, h).start()
        a_main(phase, 1, h).start()
        a_main(phase, 2, h).start()
        if far:
            a_rim(phase, 3, h, True).start()
        a_main(phase, 3, h).start()

    def gather_product(phase, i):
        s = lax.rem(y + 3 * i + 3 * ((i * (i - 1)) // 2), NCOL)
        low = jnp.where(gz > 0, window[phase, i, 0:HR], 0.0)
        high = jnp.where(gz < n_gz - 1, window[phase, i, WZ - HR : WZ], 0.0)
        hi, lo = split(jnp.concatenate([low, window[phase, i, HR : HR + ZS], high], axis=0))

        value = dot3(t_hi[s], t_lo[s], hi, lo, NT)
        if i == 0:
            q_all[...] = value
        else:
            q_all[...] += value

    def gather(phase, beside0=None, beside1=None, beside2=None):
        def product(i):
            for h in range(2):
                a_rim(phase, i, h).wait_recv()
            gather_product(phase, i)

        def forwards(h):
            for i in (1, 2):
                a_main(phase, i, h).wait_recv()
                a_rim(phase, i, h).start()

        forwards(inner)
        if beside0 is not None:
            beside0()
        forwards(outer)
        a_main(phase, 3, inner).wait_recv()
        a_rim(phase, 3, inner).start()
        product(0)
        if beside1 is not None:
            beside1()
        a_main(phase, 3, outer).wait_recv()
        if beside2 is not None:
            beside2()
        product(3)
        product(1)
        product(2)

    def rays(p):
        hi, lo = split(q_all[pl.ds(pl.multiple_of(p * PW, 128), PW)])

        def one(a, k):
            pick = lambda v: jnp.concatenate(
                [v[k * 128 : (k + 1) * 128], v[256 + k * 64 : 320 + k * 64]], axis=0
            )
            both = dot(pick(hi), jnp.concatenate([w_hi[a], w_lo[a]], axis=1), NN)
            return both[:, :128] + (both[:, 128:] + dot(pick(lo), w_hi[a], NN))

        pa = one(2 * p, 0)
        pb = one(2 * p + 1, 1)
        return jnp.concatenate([pa[:128], pb[:128], pa[128:], pb[128:]], axis=0)

    zero8 = jnp.zeros((8, 128), F32)

    def take_g0(h, value, far):
        g0[half(h, 0)] = value
        window[0, 0, half(h)] = value
        gather_start(0, h, far)

    back(0, take_g0)
    gather(0)

    def rays0(p, acc):
        x = rays(p)
        q0[p] = x
        z_of(p, x)
        return acc + squares(x)

    norm_q0 = lax.fori_loop(0, PAIRS, rays0, zero8, unroll=2)
    ar_first(0, squares(g0[...]), norm_q0)

    def take_h0(h, value, far):
        h0[half(h, 0)] = value
        window[1, 0, half(h)] = value * SCALE
        gather_start(1, h, far)

    back(1, take_h0, beside1=lambda: ar_second(0))

    def step0():
        sums = ar_get(0, 1)
        gamma = total(sums[0:1])
        alpha = gamma / total(sums[1:2])
        scalars[0:1] = jnp.broadcast_to(gamma, (1, 128))
        scalars[1:2] = jnp.broadcast_to(alpha, (1, 128))
        g1[...] = g0[...] - alpha * h0[...]
        ar_first(1, squares(g1[...]), zero8)

    def first_residual():
        alpha = scalars[1:2]

        def some(p, _):
            early, late = as_measured(q0[p])
            r1[:, early_at(p)] = meas_ref[:, early_at(p)] - alpha * early
            r1[:, late_at(p)] = meas_ref[:, late_at(p)] - alpha * late
            return 0

        lax.fori_loop(0, PAIRS, some, 0)

    gather(1, step0, first_residual, lambda: ar_second(1))
    gamma0 = scalars[0:1, 0:1]
    alpha0 = scalars[1:2, 0:1]

    def rays1(p, _):
        x = q0[p] - (alpha0 * (1.0 / SCALE)) * rays(p)
        q1[p] = x
        z_of(p, x)
        return 0

    lax.fori_loop(0, PAIRS, rays1, 0, unroll=2)

    gamma1 = total(ar_get(1, 1)[0:1])
    beta = gamma1 / gamma0

    def rays2(p, acc):
        x = q1[p] + beta * q0[p]
        q1[p] = x
        return acc + squares(x)

    ar_first(2, lax.fori_loop(0, PAIRS, rays2, zero8), zero8)

    def take_l0(h, value, _):
        l0[half(h, 0)] = value

    def image_out():
        def some(p, _):
            early, late = as_measured(q1[p])
            res_ref[:, early_at(p)] = early
            res_ref[:, late_at(p)] = late
            return 0

        lax.fori_loop(0, PAIRS, some, 0)

    back(2, take_l0, beside1=lambda: ar_second(2), beside2=image_out)
    sums = ar_get(2, 1)
    alpha1 = gamma1 / total(sums[0:1])
    grad_ref[...] = g1[...] - alpha1 * (l0[...] + beta * h0[...])
    vol_ref[...] = alpha0 * g0[...] + alpha1 * (g1[...] + beta * g0[...])
    res_ref[...] = r1[...] - alpha1 * res_ref[...]

    for phase in range(3):
        for h in range(2):
            for i in range(NCOL):
                b_rim(phase, i, h).wait_send()
            for i in range(3):
                b_direct(phase, i, h).wait_send()
    for phase in range(2):
        for h in range(2):
            for i in range(NCOL):
                a_rim(phase, i, h).wait_send()
            for i in range(1, NCOL):
                a_main(phase, i, h).wait_send()


def hand_on(a_ref, b_ref, c_ref, x_ref, y_ref, z_ref):
    x_ref[...] = a_ref[...]
    y_ref[...] = b_ref[...]
    z_ref[...] = c_ref[...]


def on_device(lo_size, measured, view_offset, tile_index, footprint, transaxial):
    hi_size = lax.axis_size("gz") // lo_size
    flat, deep = lo_size // 2 * NCOL, hi_size * 2
    vmem = pl.BlockSpec(memory_space=pltpu.VMEM)
    anywhere = pl.BlockSpec(memory_space=pl.ANY)
    smem = pl.BlockSpec(memory_space=pltpu.SMEM)
    dma = pltpu.SemaphoreType.DMA
    scratch = [
        pltpu.VMEM((NA, C, NXW), F32),
        pltpu.VMEM((NCOL, KC, VX), BF16),
        pltpu.VMEM((NCOL, KC, VX), BF16),
        pltpu.VMEM((TOP + WZ, 128), F32),
        pltpu.VMEM((NA, WZ, 128), BF16),
        pltpu.VMEM((NA, WZ, 128), BF16),
        pltpu.VMEM((2 * WZ, KC), BF16),
        pltpu.VMEM((KC, WZ), F32),
        pltpu.VMEM((PAIRS, PW, 128), F32),
        pltpu.VMEM((PAIRS, PW, 128), F32),
        pltpu.VMEM((C, 2 * NA * R), F32),
        pltpu.VMEM((3, NCOL, WZ, VX), F32),
        pltpu.VMEM((3, NCOL, 2, HR, VX), F32),
        pltpu.VMEM((3, 3, ZS, VX), F32),
        pltpu.VMEM((2, NCOL, WZ, VX), F32),
        pltpu.VMEM((ZS, VX), F32),
        pltpu.VMEM((ZS, VX), F32),
        pltpu.VMEM((ZS, VX), F32),
        pltpu.VMEM((ZS, VX), F32),
        pltpu.VMEM((8, 128), F32),
        pltpu.VMEM((3, flat, 2, 128), F32),
        pltpu.VMEM((3, deep, 2, 128), F32),
        pltpu.VMEM((C, 2 * NA * R), F32),
        dma(()),
        dma((NA,)),
        dma((3, NCOL, 2)),
        dma((3, NCOL, 2)),
        dma((3, 3, 2)),
        dma((3, 3, 2)),
        dma((2, NCOL, 2)),
        dma((2, NCOL, 2)),
        dma((2, NCOL, 2)),
        dma((2, NCOL, 2)),
        dma((3, flat + deep)),
        dma((3, flat + deep)),
    ]
    shapes = (
        jax.ShapeDtypeStruct((ZS, VX), F32),
        jax.ShapeDtypeStruct((C, 2 * NA * R), F32),
        jax.ShapeDtypeStruct((ZS, VX), F32),
    )
    outs = pl.pallas_call(
        functools.partial(kernel, lo_size),
        out_shape=shapes,
        in_specs=[smem, smem, vmem, anywhere, anywhere],
        out_specs=(vmem, vmem, vmem),
        scratch_shapes=scratch,
        compiler_params=pltpu.CompilerParams(
            collective_id=0, has_side_effects=True, vmem_limit_bytes=56 * 1024 * 1024
        ),
        cost_estimate=pl.CostEstimate(flops=12_000_000_000, bytes_accessed=9_000_000, transcendentals=0),
    )(view_offset, tile_index, jnp.swapaxes(footprint, 1, 2), measured, transaxial)
    return pl.pallas_call(
        hand_on,
        out_shape=shapes,
        in_specs=[vmem] * 3,
        out_specs=(vmem,) * 3,
        compiler_params=pltpu.CompilerParams(vmem_limit_bytes=60 * 1024 * 1024),
    )(*outs)


def solution(mesh):
    lo_size = min(8, mesh.shape["gz"] // 2)
    return jax.shard_map(
        functools.partial(on_device, lo_size),
        mesh=mesh,
        in_specs=(P("col", "gz"), P("gz"), P("gz"), P(), P(None, "col", None)),
        out_specs=(P("gz", "col"), P("col", "gz"), P("gz", "col")),
        check_vma=False,
    )
```

```python
import functools

import jax
import jax.numpy as jnp
from jax import lax
from jax.experimental import pallas as pl
from jax.experimental.pallas import tpu as pltpu
from jax.sharding import PartitionSpec as P

MESH = pl.DeviceIdType.MESH
F32 = jnp.float32
BF16 = jnp.bfloat16

NA = 8
R = 64
ZW = 32
ZS = 128
HR = 64
WZ = 256
C = 184
NXW = 1024
NCOL = 4
VX = NXW // NCOL
PAIRS = NA // 2
PW = 384
KC = PAIRS * PW
TOP = WZ - ZW
SCALE = 2.0**40
NT = (((1,), (1,)), ((), ()))
NN = (((1,), (0,)), ((), ()))


def split(x):
    hi = x.astype(BF16)
    return hi, (x - hi.astype(F32)).astype(BF16)


def dot(a, b, dims):
    return lax.dot_general(a, b, dimension_numbers=dims, preferred_element_type=F32)


def dot3(a_hi, a_lo, b_hi, b_lo, dims):
    a = jnp.concatenate([a_hi, a_lo, a_hi], axis=dims[0][0][0])
    b = jnp.concatenate([b_hi, b_hi, b_lo], axis=dims[0][1][0])
    return dot(a, b, dims)


def squares(x):
    rows, lanes = x.shape
    y = jnp.sum((x * x).reshape(rows // 8, 8, lanes), axis=0)
    return sum(y[:, k * 128 : (k + 1) * 128] for k in range(lanes // 128))


def total(x):
    return jnp.sum(x, axis=(0, 1), keepdims=True)


def kernel(
    lo_size,
    off_ref, tile_ref, foot_ref, measured_ref, trans_ref,
    vol_ref, res_ref, grad_ref,
    stage, t_hi, t_lo, shifted, w_hi, w_lo,
    z_both, q_all, q0, q1, r1,
    part, rim, direct,
    window, g0, g1, h0, h1, scalars,
    ar1, ar2,
    meas_ref, m_sem, t_sem, rim_send, rim_recv, dir_send, dir_recv,
    gat_send, gat_recv, win_send, win_recv, ar_send, ar_recv,
):
    n_gz = lax.axis_size("gz")
    hi_size = n_gz // lo_size
    x_size = lo_size // 2
    gz = lax.axis_index("gz")
    y = lax.axis_index("col")
    z_at = lax.div(gz, lo_size)
    x_at = lax.div(lax.rem(gz, lo_size), 2)
    core = lax.rem(gz, 2)
    inner, outer = 1 - core, core

    def col(d):
        return lax.rem(y + d, NCOL)

    def flat_peer(d):
        at = lax.rem(x_at * NCOL + y + d, x_size * NCOL)
        return (z_at * lo_size + lax.div(at, NCOL) * 2 + core, lax.rem(at, NCOL))

    def deep_peer(d):
        at = lax.rem(z_at * 2 + core + d, hi_size * 2)
        return (lax.div(at, 2) * lo_size + x_at * 2 + lax.rem(at, 2), y)

    groups = ((x_size * NCOL, flat_peer), (hi_size * 2, deep_peer))

    barrier = pltpu.get_barrier_semaphore()

    def greet(to):
        pl.semaphore_signal(barrier, inc=1, device_id=to, device_id_type=MESH)

    for size, peer in groups:
        lax.fori_loop(1, size, lambda d, c, peer=peer: (greet(peer(d)), c)[1], 0)
    for other in (1, n_gz - 1):
        greet((lax.rem(gz + other, n_gz), y))
        greet((lax.rem(gz + other, n_gz), col(2)))
    greeted = groups[0][0] + groups[1][0] + 2

    def owner(i):
        return lax.rem(y + 2 + 3 * i + 3 * lax.div(i * (i - 1), 2), NCOL)

    def t_load(i):
        cols = pl.ds(pl.multiple_of(owner(i) * VX, VX), VX)
        return pltpu.make_async_copy(trans_ref.at[:, :, cols], stage.at[i], t_sem.at[i])

    loads = [t_load(i) for i in range(NCOL)]
    meas_load = pltpu.make_async_copy(measured_ref, meas_ref, m_sem)
    meas_load.start()
    for load in loads:
        load.start()

    lane = lax.broadcasted_iota(jnp.int32, (1, 128), 1)
    first_half = lane < 64

    shifted[...] = jnp.zeros_like(shifted)

    def place(a, _):
        shifted[TOP:WZ, :] = jnp.concatenate(
            [foot_ref[tile_ref[a]], foot_ref[tile_ref[a + NA]]], axis=1
        )
        one = shifted[pl.ds(TOP - off_ref[a], WZ), :]
        two = shifted[pl.ds(TOP - off_ref[a + NA], WZ), :]
        hi, lo = split(jnp.where(first_half, one, two))
        w_hi[a] = hi
        w_lo[a] = lo
        return 0

    lax.fori_loop(0, NA, place, 0)

    def z_of(p, x):
        hi, lo = split(x)
        pick = lambda v, k: jnp.concatenate([v[k * 128 : (k + 1) * 128], v[256:]], axis=0)
        za = dot3(w_hi[2 * p], w_lo[2 * p], pick(hi, 0), pick(lo, 0), NT)
        zb = dot3(w_hi[2 * p + 1], w_lo[2 * p + 1], pick(hi, 1), pick(lo, 1), NT)
        third = jnp.where(first_half, za[:, 128:], zb[:, 128:])
        hi, lo = split(jnp.concatenate([za[:, :128], zb[:, :128], third], axis=1))
        at = pl.ds(pl.multiple_of(p * PW, 128), PW)
        z_both[0:WZ, at] = hi
        z_both[WZ:, at] = lo

    def early_at(p):
        return pl.ds(pl.multiple_of(p * 128, 128), 128)

    def late_at(p):
        return pl.ds(pl.multiple_of(NA * R + p * 128, 128), 128)

    def z_of_measured(p, _):
        early = meas_ref[:, early_at(p)]
        late = meas_ref[:, late_at(p)]
        a = jnp.where(first_half, early, pltpu.roll(late, 64, 1))
        b = jnp.where(first_half, pltpu.roll(early, 64, 1), late)
        gap = jnp.zeros((8, 128), F32)
        z_of(p, jnp.concatenate([a[:128], b[:128], a[128:], gap, b[128:], gap], axis=0))
        return 0

    def as_measured(x):
        a = jnp.concatenate([x[0:128], x[256:312]], axis=0)
        b = jnp.concatenate([x[128:256], x[320:376]], axis=0)
        early = jnp.where(first_half, a, pltpu.roll(b, 64, 1))
        late = jnp.where(first_half, pltpu.roll(a, 64, 1), b)
        return early, late

    meas_load.wait()
    lax.fori_loop(0, PAIRS, z_of_measured, 0)

    def convert(i, s):
        t_load(i).wait()

        def some(p, _):
            base = p * PW
            for h in range(2):
                x = stage[i, 2 * p + h]
                hi, lo = split(x[:128])
                at = pl.ds(pl.multiple_of(base + h * 128, 64), 128)
                t_hi[s, at] = hi
                t_lo[s, at] = lo
                hi, lo = split(jnp.concatenate([x[128:], jnp.zeros((8, VX), F32)], axis=0))
                at = pl.ds(pl.multiple_of(base + 256 + h * 64, 64), 64)
                t_hi[s, at] = hi
                t_lo[s, at] = lo
            return 0

        lax.fori_loop(0, PAIRS, some, 0)

    pl.semaphore_wait(barrier, greeted)

    def remote(src, dst, send, recv, to):
        return pltpu.make_async_remote_copy(
            src_ref=src, dst_ref=dst, send_sem=send, recv_sem=recv, device_id=to, device_id_type=MESH
        )

    ar_bufs = (ar1, ar2)
    ar_at = (x_at * NCOL + y, z_at * 2 + core)

    def ar_put(k, level, value):
        size, peer = groups[level]
        slot = ar_bufs[level].at[k, ar_at[level]]
        slot[...] = value
        for d in range(1, size):
            remote(slot, slot, ar_send.at[k, level], ar_recv.at[k, level], peer(d)).start()

    def ar_get(k, level):
        size, peer = groups[level]
        others = ar_bufs[level].at[k, pl.ds(0, size - 1)]
        every = remote(others, others, ar_send.at[k, level], ar_recv.at[k, level], peer(1))
        every.wait_recv()
        every.wait_send()
        return jnp.sum(ar_bufs[level][k], axis=0)

    def ar_first(k, one, two):
        rows = [jnp.sum(v, axis=0, keepdims=True) for v in (one, two)]
        ar_put(k, 0, jnp.concatenate(rows, axis=0))

    def ar_second(k):
        ar_put(k, 1, ar_get(k, 0))

    def half(h, base=HR):
        return pl.ds(pl.multiple_of(base + h * 64, 64), 64)

    def edge(h):
        return pl.ds(pl.multiple_of((1 - h) * (WZ - HR), 64), HR)

    def b_rim(phase, i, h):
        return remote(
            part.at[phase, i, edge(h)], rim.at[phase, i, h],
            rim_send.at[phase, i, h], rim_recv.at[phase, i, h],
            (lax.rem(gz + n_gz + 1 - 2 * h, n_gz), y),
        )

    def b_direct(phase, i, h):
        return remote(
            part.at[phase, i, half(h)], direct.at[phase, i, half(h, 0)],
            dir_send.at[phase, i, h], dir_recv.at[phase, i, h], (gz, owner(i)),
        )

    def with_rim(phase, i, h):
        b_rim(phase, i, h).wait_recv()
        inside = jnp.where(h == 0, gz > 0, gz < n_gz - 1)
        return part[phase, i, half(h)] + jnp.where(inside, rim[phase, i, h], 0.0)

    def send_half(phase, i, h):
        part[phase, i, half(h)] = with_rim(phase, i, h)
        b_direct(phase, i, h).start()

    def back(phase, take, beside1=None, beside2=None):
        def product(i, _):
            s = owner(i)
            if phase == 0:
                convert(i, s)
            both = dot(z_both[...], t_hi[s], NN)
            part[phase, i] = both[0:WZ] + (both[WZ:] + dot(z_both[0:WZ], t_lo[s], NN))
            b_rim(phase, i, inner).start()
            b_rim(phase, i, outer).start()

            @pl.when(i > 0)
            def _():
                send_half(phase, i - 1, inner)

            return 0

        lax.fori_loop(0, NCOL, product, 0)
        send_half(phase, 0, outer)
        send_half(phase, 1, outer)
        if beside1 is not None:
            beside1()
        send_half(phase, 2, outer)
        if beside2 is not None:
            beside2()
        for h, far in ((inner, False), (outer, True)):
            own = with_rim(phase, 3, h)
            for i in range(3):
                b_direct(phase, i, h).wait_recv()
            d = [direct[phase, i, half(h, 0)] for i in range(3)]
            take(h, own + (d[0] + (d[1] + d[2])), far)

    def a_main(phase, i, h):
        return remote(
            window.at[phase, 0, half(h)], window.at[phase, i, half(h)],
            gat_send.at[phase, i, h], gat_recv.at[phase, i, h],
            (gz, lax.rem(y + i + lax.div(i, 2) + 2 * lax.div(i, 3), NCOL)),
        )

    def a_rim(phase, i, h, far=False):
        src = window.at[phase, 0 if far else i, half(h)]
        return remote(
            src, window.at[phase, i, edge(h)],
            win_send.at[phase, i, h], win_recv.at[phase, i, h],
            (lax.rem(gz + n_gz - 1 + 2 * h, n_gz), col(2) if far else y),
        )

    def gather_start(phase, h, far):
        a_rim(phase, 0, h).start()
        a_main(phase, 1, h).start()
        a_main(phase, 2, h).start()
        if far:
            a_rim(phase, 3, h, True).start()
        a_main(phase, 3, h).start()

    def gather_product(phase, i):
        s = lax.rem(y + 3 * i + 3 * ((i * (i - 1)) // 2), NCOL)
        low = jnp.where(gz > 0, window[phase, i, 0:HR], 0.0)
        high = jnp.where(gz < n_gz - 1, window[phase, i, WZ - HR : WZ], 0.0)
        hi, lo = split(jnp.concatenate([low, window[phase, i, HR : HR + ZS], high], axis=0))

        value = dot3(t_hi[s], t_lo[s], hi, lo, NT)
        if i == 0:
            q_all[...] = value
        else:
            q_all[...] += value

    def gather(phase, beside0=None, beside1=None, beside2=None):
        def product(i):
            for h in range(2):
                a_rim(phase, i, h).wait_recv()
            gather_product(phase, i)

        def forwards(h):
            for i in (1, 2):
                a_main(phase, i, h).wait_recv()
                a_rim(phase, i, h).start()

        forwards(inner)
        if beside0 is not None:
            beside0()
        forwards(outer)
        a_main(phase, 3, inner).wait_recv()
        a_rim(phase, 3, inner).start()
        product(0)
        if beside1 is not None:
            beside1()
        a_main(phase, 3, outer).wait_recv()
        if beside2 is not None:
            beside2()
        product(3)
        product(1)
        product(2)

    def rays(p):
        hi, lo = split(q_all[pl.ds(pl.multiple_of(p * PW, 128), PW)])

        def one(a, k):
            pick = lambda v: jnp.concatenate(
                [v[k * 128 : (k + 1) * 128], v[256 + k * 64 : 320 + k * 64]], axis=0
            )
            both = dot(pick(hi), jnp.concatenate([w_hi[a], w_lo[a]], axis=1), NN)
            return both[:, :128] + (both[:, 128:] + dot(pick(lo), w_hi[a], NN))

        pa = one(2 * p, 0)
        pb = one(2 * p + 1, 1)
        return jnp.concatenate([pa[:128], pb[:128], pa[128:], pb[128:]], axis=0)

    zero8 = jnp.zeros((8, 128), F32)

    def take_g0(h, value, far):
        g0[half(h, 0)] = value
        window[0, 0, half(h)] = value
        gather_start(0, h, far)

    back(0, take_g0)
    gather(0)

    def rays0(p, acc):
        x = rays(p)
        q0[p] = x
        return acc + squares(x)

    def z_of_rays(q):
        lax.fori_loop(0, PAIRS, lambda p, c: (z_of(p, q[p]), c)[1], 0, unroll=2)

    norm_q0 = lax.fori_loop(0, PAIRS, rays0, zero8, unroll=2)
    ar_first(0, squares(g0[...]), norm_q0)
    z_of_rays(q0)

    def take_h0(h, value, far):
        h0[half(h, 0)] = value
        window[1, 0, half(h)] = value * SCALE
        gather_start(1, h, far)

    back(1, take_h0, beside1=lambda: ar_second(0))

    def step0():
        sums = ar_get(0, 1)
        gamma = total(sums[0:1])
        alpha = gamma / total(sums[1:2])
        scalars[0:1] = jnp.broadcast_to(gamma, (1, 128))
        scalars[1:2] = jnp.broadcast_to(alpha, (1, 128))
        g1[...] = g0[...] - alpha * h0[...]
        ar_first(1, squares(g1[...]), zero8)

    gather(1, step0, None, lambda: ar_second(1))
    gamma0 = scalars[0:1, 0:1]
    alpha0 = scalars[1:2, 0:1]

    def rays1(p, _):
        q1[p] = q0[p] - (alpha0 * (1.0 / SCALE)) * rays(p)
        return 0

    lax.fori_loop(0, PAIRS, rays1, 0, unroll=2)

    gamma1 = total(ar_get(1, 1)[0:1])
    beta = gamma1 / gamma0

    def rays2(p, acc):
        x = q1[p] + beta * q0[p]
        q1[p] = x
        return acc + squares(x)

    ar_first(2, lax.fori_loop(0, PAIRS, rays2, zero8), zero8)
    z_of_rays(q1)

    def take_h1(h, value, _):
        h1[half(h, 0)] = value

    def residual_parts():
        def some(p, _):
            for at, x0, x1 in zip((early_at(p), late_at(p)), as_measured(q0[p]), as_measured(q1[p])):
                r1[:, at] = meas_ref[:, at] - alpha0 * x0
                res_ref[:, at] = x1
            return 0

        lax.fori_loop(0, PAIRS, some, 0)

    back(2, take_h1, beside1=lambda: ar_second(2), beside2=residual_parts)
    sums = ar_get(2, 1)
    alpha1 = gamma1 / total(sums[0:1])
    grad_ref[...] = g1[...] - alpha1 * h1[...]
    vol_ref[...] = alpha0 * g0[...] + alpha1 * (g1[...] + beta * g0[...])
    res_ref[...] = r1[...] - alpha1 * res_ref[...]

    for phase in range(3):
        for h in range(2):
            for i in range(NCOL):
                b_rim(phase, i, h).wait_send()
            for i in range(3):
                b_direct(phase, i, h).wait_send()
    for phase in range(2):
        for h in range(2):
            for i in range(NCOL):
                a_rim(phase, i, h).wait_send()
            for i in range(1, NCOL):
                a_main(phase, i, h).wait_send()


def hand_on(v_ref, r_ref, g_ref, v_out, r_out, g_out, v, r, g, sem_in, sem_out):
    cut = C // 2 // 8 * 8
    pieces = [(r_ref.at[0:cut], r.at[0:cut], r_out.at[0:cut]), (r_ref.at[cut:], r.at[cut:], r_out.at[cut:])]
    pieces += [(v_ref, v, v_out), (g_ref, g, g_out)]
    ins = [pltpu.make_async_copy(a, b, sem_in.at[k]) for k, (a, b, _) in enumerate(pieces)]
    outs = [pltpu.make_async_copy(b, c, sem_out.at[k]) for k, (_, b, c) in enumerate(pieces)]
    for copy in ins:
        copy.start()
    for arrived, copy in zip(ins, outs):
        arrived.wait()
        copy.start()
    for copy in outs:
        copy.wait()


def on_device(lo_size, measured, view_offset, tile_index, footprint, transaxial):
    hi_size = lax.axis_size("gz") // lo_size
    flat, deep = lo_size // 2 * NCOL, hi_size * 2
    vmem = pl.BlockSpec(memory_space=pltpu.VMEM)
    anywhere = pl.BlockSpec(memory_space=pl.ANY)
    smem = pl.BlockSpec(memory_space=pltpu.SMEM)
    dma = pltpu.SemaphoreType.DMA
    scratch = [
        pltpu.VMEM((NCOL, NA, C, VX), F32),
        pltpu.VMEM((NCOL, KC, VX), BF16),
        pltpu.VMEM((NCOL, KC, VX), BF16),
        pltpu.VMEM((TOP + WZ, 128), F32),
        pltpu.VMEM((NA, WZ, 128), BF16),
        pltpu.VMEM((NA, WZ, 128), BF16),
        pltpu.VMEM((2 * WZ, KC), BF16),
        pltpu.VMEM((KC, WZ), F32),
        pltpu.VMEM((PAIRS, PW, 128), F32),
        pltpu.VMEM((PAIRS, PW, 128), F32),
        pltpu.VMEM((C, 2 * NA * R), F32),
        pltpu.VMEM((3, NCOL, WZ, VX), F32),
        pltpu.VMEM((3, NCOL, 2, HR, VX), F32),
        pltpu.VMEM((3, 3, ZS, VX), F32),
        pltpu.VMEM((2, NCOL, WZ, VX), F32),
        pltpu.VMEM((ZS, VX), F32),
        pltpu.VMEM((ZS, VX), F32),
        pltpu.VMEM((ZS, VX), F32),
        pltpu.VMEM((ZS, VX), F32),
        pltpu.VMEM((8, 128), F32),
        pltpu.VMEM((3, flat, 2, 128), F32),
        pltpu.VMEM((3, deep, 2, 128), F32),
        pltpu.VMEM((C, 2 * NA * R), F32),
        dma(()),
        dma((NCOL,)),
        dma((3, NCOL, 2)),
        dma((3, NCOL, 2)),
        dma((3, 3, 2)),
        dma((3, 3, 2)),
        dma((2, NCOL, 2)),
        dma((2, NCOL, 2)),
        dma((2, NCOL, 2)),
        dma((2, NCOL, 2)),
        dma((3, 2)),
        dma((3, 2)),
    ]
    shapes = (
        jax.ShapeDtypeStruct((ZS, VX), F32),
        jax.ShapeDtypeStruct((C, 2 * NA * R), F32),
        jax.ShapeDtypeStruct((ZS, VX), F32),
    )
    outs = pl.pallas_call(
        functools.partial(kernel, lo_size),
        out_shape=shapes,
        in_specs=[smem, smem, vmem, anywhere, anywhere],
        out_specs=(vmem, vmem, vmem),
        scratch_shapes=scratch,
        compiler_params=pltpu.CompilerParams(
            collective_id=0, has_side_effects=True, vmem_limit_bytes=56 * 1024 * 1024
        ),
        cost_estimate=pl.CostEstimate(flops=12_000_000_000, bytes_accessed=9_000_000, transcendentals=0),
    )(view_offset, tile_index, jnp.swapaxes(footprint, 1, 2), measured, transaxial)
    return pl.pallas_call(
        hand_on,
        out_shape=shapes,
        in_specs=[anywhere] * 3,
        out_specs=(anywhere,) * 3,
        scratch_shapes=[pltpu.VMEM(shape.shape, F32) for shape in shapes] + [dma((4,)), dma((4,))],
        compiler_params=pltpu.CompilerParams(vmem_limit_bytes=60 * 1024 * 1024),
    )(*outs)


def solution(mesh):
    lo_size = min(8, mesh.shape["gz"] // 2)
    return jax.shard_map(
        functools.partial(on_device, lo_size),
        mesh=mesh,
        in_specs=(P("col", "gz"), P("gz"), P("gz"), P(), P(None, "col", None)),
        out_specs=(P("gz", "col"), P("col", "gz"), P("gz", "col")),
        check_vma=False,
    )
```

```python
import functools

import jax
import jax.numpy as jnp
from jax import lax
from jax.experimental import pallas as pl
from jax.experimental.pallas import tpu as pltpu
from jax.sharding import PartitionSpec as P

MESH = pl.DeviceIdType.MESH
F32 = jnp.float32
BF16 = jnp.bfloat16

NA = 8
R = 64
ZW = 32
ZS = 128
HR = 64
WZ = 256
C = 184
NXW = 1024
NCOL = 4
VX = NXW // NCOL
PAIRS = NA // 2
PW = 384
KC = PAIRS * PW
TOP = WZ - ZW
SCALE = 2.0**40
NT = (((1,), (1,)), ((), ()))
NN = (((1,), (0,)), ((), ()))


def split(x):
    hi = x.astype(BF16)
    return hi, (x - hi.astype(F32)).astype(BF16)


def dot(a, b, dims):
    return lax.dot_general(a, b, dimension_numbers=dims, preferred_element_type=F32)


def dot3(a_hi, a_lo, b_hi, b_lo, dims):
    a = jnp.concatenate([a_hi, a_lo, a_hi], axis=dims[0][0][0])
    b = jnp.concatenate([b_hi, b_hi, b_lo], axis=dims[0][1][0])
    return dot(a, b, dims)


def squares(x):
    rows, lanes = x.shape
    y = jnp.sum((x * x).reshape(rows // 8, 8, lanes), axis=0)
    return sum(y[:, k * 128 : (k + 1) * 128] for k in range(lanes // 128))


def total(x):
    return jnp.sum(x, axis=(0, 1), keepdims=True)


def kernel(
    lo_size,
    off_ref, tile_ref, foot_ref, measured_ref, trans_ref,
    vol_ref, res_ref, grad_ref,
    stage, t_hi, t_lo, shifted, w_hi, w_lo,
    z_both, q_all, q0, q1, r1,
    part, rim, direct,
    window, g0, g1, h0, h1, scalars,
    ar1, ar2,
    meas_ref, m_sem, t_sem, rim_send, rim_recv, dir_send, dir_recv,
    gat_send, gat_recv, win_send, win_recv, ar_send, ar_recv,
):
    n_gz = lax.axis_size("gz")
    hi_size = n_gz // lo_size
    x_size = lo_size // 2
    gz = lax.axis_index("gz")
    y = lax.axis_index("col")
    z_at = lax.div(gz, lo_size)
    x_at = lax.div(lax.rem(gz, lo_size), 2)
    core = lax.rem(gz, 2)
    inner, outer = 1 - core, core

    def col(d):
        return lax.rem(y + d, NCOL)

    def flat_peer(d):
        at = lax.rem(x_at * NCOL + y + d, x_size * NCOL)
        return (z_at * lo_size + lax.div(at, NCOL) * 2 + core, lax.rem(at, NCOL))

    def deep_peer(d):
        at = lax.rem(z_at * 2 + core + d, hi_size * 2)
        return (lax.div(at, 2) * lo_size + x_at * 2 + lax.rem(at, 2), y)

    groups = ((x_size * NCOL, flat_peer), (hi_size * 2, deep_peer))

    barrier = pltpu.get_barrier_semaphore()

    def greet(to):
        pl.semaphore_signal(barrier, inc=1, device_id=to, device_id_type=MESH)

    def owner(i):
        return lax.rem(y + 2 + 3 * i + 3 * lax.div(i * (i - 1), 2), NCOL)

    def t_load(i):
        cols = pl.ds(pl.multiple_of(owner(i) * VX, VX), VX)
        return pltpu.make_async_copy(trans_ref.at[:, :, cols], stage.at[i], t_sem.at[i])

    loads = [t_load(i) for i in range(NCOL)]
    meas_load = pltpu.make_async_copy(measured_ref, meas_ref, m_sem)
    meas_load.start()
    for load in loads:
        load.start()

    for other in (1, n_gz - 1):
        greet((lax.rem(gz + other, n_gz), y))
        greet((lax.rem(gz + other, n_gz), col(2)))
    for size, peer in groups:
        for d in range(1, size):
            greet(peer(d))
    greeted = groups[0][0] + groups[1][0] + 2

    lane = lax.broadcasted_iota(jnp.int32, (1, 128), 1)
    first_half = lane < 64

    shifted[...] = jnp.zeros_like(shifted)

    def place(a, _):
        shifted[TOP:WZ, :] = jnp.concatenate(
            [foot_ref[tile_ref[a]], foot_ref[tile_ref[a + NA]]], axis=1
        )
        one = shifted[pl.ds(TOP - off_ref[a], WZ), :]
        two = shifted[pl.ds(TOP - off_ref[a + NA], WZ), :]
        hi, lo = split(jnp.where(first_half, one, two))
        w_hi[a] = hi
        w_lo[a] = lo
        return 0

    lax.fori_loop(0, NA, place, 0)

    def z_of(p, x):
        hi, lo = split(x)
        pick = lambda v, k: jnp.concatenate([v[k * 128 : (k + 1) * 128], v[256:]], axis=0)
        za = dot3(w_hi[2 * p], w_lo[2 * p], pick(hi, 0), pick(lo, 0), NT)
        zb = dot3(w_hi[2 * p + 1], w_lo[2 * p + 1], pick(hi, 1), pick(lo, 1), NT)
        third = jnp.where(first_half, za[:, 128:], zb[:, 128:])
        hi, lo = split(jnp.concatenate([za[:, :128], zb[:, :128], third], axis=1))
        at = pl.ds(pl.multiple_of(p * PW, 128), PW)
        z_both[0:WZ, at] = hi
        z_both[WZ:, at] = lo

    def early_at(p):
        return pl.ds(pl.multiple_of(p * 128, 128), 128)

    def late_at(p):
        return pl.ds(pl.multiple_of(NA * R + p * 128, 128), 128)

    def z_of_measured(p, _):
        early = meas_ref[:, early_at(p)]
        late = meas_ref[:, late_at(p)]
        a = jnp.where(first_half, early, pltpu.roll(late, 64, 1))
        b = jnp.where(first_half, pltpu.roll(early, 64, 1), late)
        gap = jnp.zeros((8, 128), F32)
        z_of(p, jnp.concatenate([a[:128], b[:128], a[128:], gap, b[128:], gap], axis=0))
        return 0

    def as_measured(x):
        a = jnp.concatenate([x[0:128], x[256:312]], axis=0)
        b = jnp.concatenate([x[128:256], x[320:376]], axis=0)
        early = jnp.where(first_half, a, pltpu.roll(b, 64, 1))
        late = jnp.where(first_half, pltpu.roll(a, 64, 1), b)
        return early, late

    meas_load.wait()
    lax.fori_loop(0, PAIRS, z_of_measured, 0, unroll=2)

    def convert(i, s):
        t_load(i).wait()

        def some(p, _):
            base = p * PW
            for h in range(2):
                x = stage[i, 2 * p + h]
                hi, lo = split(x[:128])
                at = pl.ds(pl.multiple_of(base + h * 128, 64), 128)
                t_hi[s, at] = hi
                t_lo[s, at] = lo
                hi, lo = split(jnp.concatenate([x[128:], jnp.zeros((8, VX), F32)], axis=0))
                at = pl.ds(pl.multiple_of(base + 256 + h * 64, 64), 64)
                t_hi[s, at] = hi
                t_lo[s, at] = lo
            return 0

        lax.fori_loop(0, PAIRS, some, 0)

    pl.semaphore_wait(barrier, greeted)

    def remote(src, dst, send, recv, to):
        return pltpu.make_async_remote_copy(
            src_ref=src, dst_ref=dst, send_sem=send, recv_sem=recv, device_id=to, device_id_type=MESH
        )

    ar_bufs = (ar1, ar2)
    ar_at = (x_at * NCOL + y, z_at * 2 + core)

    def ar_put(k, level, value):
        size, peer = groups[level]
        slot = ar_bufs[level].at[k, ar_at[level]]
        slot[...] = value
        for d in range(1, size):
            remote(slot, slot, ar_send.at[k, level], ar_recv.at[k, level], peer(d)).start()

    def ar_get(k, level):
        size, peer = groups[level]
        others = ar_bufs[level].at[k, pl.ds(0, size - 1)]
        every = remote(others, others, ar_send.at[k, level], ar_recv.at[k, level], peer(1))
        every.wait_recv()
        every.wait_send()
        return jnp.sum(ar_bufs[level][k], axis=0)

    def ar_first(k, one, two):
        rows = [jnp.sum(v, axis=0, keepdims=True) for v in (one, two)]
        ar_put(k, 0, jnp.concatenate(rows, axis=0))

    def ar_second(k):
        ar_put(k, 1, ar_get(k, 0))

    def half(h, base=HR):
        return pl.ds(pl.multiple_of(base + h * 64, 64), 64)

    def edge(h):
        return pl.ds(pl.multiple_of((1 - h) * (WZ - HR), 64), HR)

    def b_rim(phase, i, h):
        return remote(
            part.at[phase, i, edge(h)], rim.at[phase, i, h],
            rim_send.at[phase, i, h], rim_recv.at[phase, i, h],
            (lax.rem(gz + n_gz + 1 - 2 * h, n_gz), y),
        )

    def b_direct(phase, i, h):
        return remote(
            part.at[phase, i, half(h)], direct.at[phase, i, half(h, 0)],
            dir_send.at[phase, i, h], dir_recv.at[phase, i, h], (gz, owner(i)),
        )

    def with_rim(phase, i, h):
        b_rim(phase, i, h).wait_recv()
        inside = jnp.where(h == 0, gz > 0, gz < n_gz - 1)
        return part[phase, i, half(h)] + jnp.where(inside, rim[phase, i, h], 0.0)

    def send_half(phase, i, h):
        part[phase, i, half(h)] = with_rim(phase, i, h)
        b_direct(phase, i, h).start()

    def back(phase, take, beside1=None, beside2=None):
        def product(i, _):
            s = owner(i)
            if phase == 0:
                convert(i, s)
            both = dot(z_both[...], t_hi[s], NN)
            part[phase, i] = both[0:WZ] + (both[WZ:] + dot(z_both[0:WZ], t_lo[s], NN))
            b_rim(phase, i, inner).start()
            b_rim(phase, i, outer).start()

            @pl.when(i > 0)
            def _():
                send_half(phase, i - 1, inner)

            return 0

        lax.fori_loop(0, NCOL, product, 0)
        send_half(phase, 0, outer)
        send_half(phase, 1, outer)
        if beside1 is not None:
            beside1()
        send_half(phase, 2, outer)
        if beside2 is not None:
            beside2()
        for h, far in ((inner, False), (outer, True)):
            own = with_rim(phase, 3, h)
            for i in range(3):
                b_direct(phase, i, h).wait_recv()
            d = [direct[phase, i, half(h, 0)] for i in range(3)]
            take(h, own + (d[0] + (d[1] + d[2])), far)

    def a_main(phase, i, h):
        return remote(
            window.at[phase, 0, half(h)], window.at[phase, i, half(h)],
            gat_send.at[phase, i, h], gat_recv.at[phase, i, h],
            (gz, lax.rem(y + i + lax.div(i, 2) + 2 * lax.div(i, 3), NCOL)),
        )

    def a_rim(phase, i, h, far=False):
        src = window.at[phase, 0 if far else i, half(h)]
        return remote(
            src, window.at[phase, i, edge(h)],
            win_send.at[phase, i, h], win_recv.at[phase, i, h],
            (lax.rem(gz + n_gz - 1 + 2 * h, n_gz), col(2) if far else y),
        )

    def gather_start(phase, h, far):
        a_rim(phase, 0, h).start()
        a_main(phase, 1, h).start()
        a_main(phase, 2, h).start()
        if far:
            a_rim(phase, 3, h, True).start()
        a_main(phase, 3, h).start()

    def gather_product(phase, i):
        s = lax.rem(y + 3 * i + 3 * ((i * (i - 1)) // 2), NCOL)
        low = jnp.where(gz > 0, window[phase, i, 0:HR], 0.0)
        high = jnp.where(gz < n_gz - 1, window[phase, i, WZ - HR : WZ], 0.0)
        hi, lo = split(jnp.concatenate([low, window[phase, i, HR : HR + ZS], high], axis=0))

        value = dot3(t_hi[s], t_lo[s], hi, lo, NT)
        if i == 0:
            q_all[...] = value
        else:
            q_all[...] += value

    def gather(phase, beside0=None, beside1=None, beside2=None):
        def product(i):
            for h in range(2):
                a_rim(phase, i, h).wait_recv()
            gather_product(phase, i)

        def forwards(h):
            for i in (1, 2):
                a_main(phase, i, h).wait_recv()
                a_rim(phase, i, h).start()

        forwards(inner)
        if beside0 is not None:
            beside0()
        forwards(outer)
        a_main(phase, 3, inner).wait_recv()
        a_rim(phase, 3, inner).start()
        product(0)
        if beside1 is not None:
            beside1()
        a_main(phase, 3, outer).wait_recv()
        if beside2 is not None:
            beside2()
        product(3)
        product(1)
        product(2)

    def rays(p):
        hi, lo = split(q_all[pl.ds(pl.multiple_of(p * PW, 128), PW)])

        def one(a, k):
            pick = lambda v: jnp.concatenate(
                [v[k * 128 : (k + 1) * 128], v[256 + k * 64 : 320 + k * 64]], axis=0
            )
            both = dot(pick(hi), jnp.concatenate([w_hi[a], w_lo[a]], axis=1), NN)
            return both[:, :128] + (both[:, 128:] + dot(pick(lo), w_hi[a], NN))

        pa = one(2 * p, 0)
        pb = one(2 * p + 1, 1)
        return jnp.concatenate([pa[:128], pb[:128], pa[128:], pb[128:]], axis=0)

    zero8 = jnp.zeros((8, 128), F32)

    def take_g0(h, value, far):
        g0[half(h, 0)] = value
        window[0, 0, half(h)] = value
        gather_start(0, h, far)

    back(0, take_g0)
    gather(0)

    def rays0(p, acc):
        x = rays(p)
        q0[p] = x
        return acc + squares(x)

    def z_of_rays(q):
        lax.fori_loop(0, PAIRS, lambda p, c: (z_of(p, q[p]), c)[1], 0, unroll=4)

    norm_q0 = lax.fori_loop(0, PAIRS, rays0, zero8, unroll=2)
    ar_first(0, squares(g0[...]), norm_q0)
    z_of_rays(q0)

    def take_h0(h, value, far):
        h0[half(h, 0)] = value
        window[1, 0, half(h)] = value * SCALE
        gather_start(1, h, far)

    back(1, take_h0, beside1=lambda: ar_second(0))

    def step0():
        sums = ar_get(0, 1)
        gamma = total(sums[0:1])
        alpha = gamma / total(sums[1:2])
        scalars[0:1] = jnp.broadcast_to(gamma, (1, 128))
        scalars[1:2] = jnp.broadcast_to(alpha, (1, 128))
        g1[...] = g0[...] - alpha * h0[...]
        ar_first(1, squares(g1[...]), zero8)

    gather(1, step0, None, lambda: ar_second(1))
    gamma0 = scalars[0:1, 0:1]
    alpha0 = scalars[1:2, 0:1]

    def rays1(p, _):
        q1[p] = q0[p] - (alpha0 * (1.0 / SCALE)) * rays(p)
        return 0

    lax.fori_loop(0, PAIRS, rays1, 0, unroll=2)

    gamma1 = total(ar_get(1, 1)[0:1])
    beta = gamma1 / gamma0

    def rays2(p, acc):
        x = q1[p] + beta * q0[p]
        q1[p] = x
        return acc + squares(x)

    ar_first(2, lax.fori_loop(0, PAIRS, rays2, zero8), zero8)
    z_of_rays(q1)

    def take_h1(h, value, _):
        h1[half(h, 0)] = value

    def sent_directs(phase):
        for h in range(2):
            for i in range(3):
                b_direct(phase, i, h).wait_send()

    def sent_earlier():
        for phase in range(2):
            sent_directs(phase)
            for h in range(2):
                for i in range(NCOL):
                    a_rim(phase, i, h).wait_send()
                for i in range(1, NCOL):
                    a_main(phase, i, h).wait_send()
        for phase in range(3):
            for h in range(2):
                for i in range(NCOL):
                    b_rim(phase, i, h).wait_send()

    def residual_parts():
        def some(p, _):
            for at, x0, x1 in zip((early_at(p), late_at(p)), as_measured(q0[p]), as_measured(q1[p])):
                r1[:, at] = meas_ref[:, at] - alpha0 * x0
                res_ref[:, at] = x1
            return 0

        lax.fori_loop(0, PAIRS, some, 0)
        sent_earlier()

    back(2, take_h1, beside1=lambda: ar_second(2), beside2=residual_parts)
    sums = ar_get(2, 1)
    alpha1 = gamma1 / total(sums[0:1])
    grad_ref[...] = g1[...] - alpha1 * h1[...]
    vol_ref[...] = alpha0 * g0[...] + alpha1 * (g1[...] + beta * g0[...])
    res_ref[...] = r1[...] - alpha1 * res_ref[...]

    sent_directs(2)


def hand_on(v_ref, r_ref, g_ref, v_out, r_out, g_out, v, r, g, sem_in, sem_out):
    cut = C // 2 // 8 * 8
    pieces = [(r_ref.at[0:cut], r.at[0:cut], r_out.at[0:cut]), (r_ref.at[cut:], r.at[cut:], r_out.at[cut:])]
    pieces += [(v_ref, v, v_out), (g_ref, g, g_out)]
    ins = [pltpu.make_async_copy(a, b, sem_in.at[k]) for k, (a, b, _) in enumerate(pieces)]
    outs = [pltpu.make_async_copy(b, c, sem_out.at[k]) for k, (_, b, c) in enumerate(pieces)]
    for copy in ins:
        copy.start()
    for arrived, copy in zip(ins, outs):
        arrived.wait()
        copy.start()
    for copy in outs:
        copy.wait()


def on_device(lo_size, measured, view_offset, tile_index, footprint, transaxial):
    hi_size = lax.axis_size("gz") // lo_size
    flat, deep = lo_size // 2 * NCOL, hi_size * 2
    vmem = pl.BlockSpec(memory_space=pltpu.VMEM)
    anywhere = pl.BlockSpec(memory_space=pl.ANY)
    smem = pl.BlockSpec(memory_space=pltpu.SMEM)
    dma = pltpu.SemaphoreType.DMA
    scratch = [
        pltpu.VMEM((NCOL, NA, C, VX), F32),
        pltpu.VMEM((NCOL, KC, VX), BF16),
        pltpu.VMEM((NCOL, KC, VX), BF16),
        pltpu.VMEM((TOP + WZ, 128), F32),
        pltpu.VMEM((NA, WZ, 128), BF16),
        pltpu.VMEM((NA, WZ, 128), BF16),
        pltpu.VMEM((2 * WZ, KC), BF16),
        pltpu.VMEM((KC, WZ), F32),
        pltpu.VMEM((PAIRS, PW, 128), F32),
        pltpu.VMEM((PAIRS, PW, 128), F32),
        pltpu.VMEM((C, 2 * NA * R), F32),
        pltpu.VMEM((3, NCOL, WZ, VX), F32),
        pltpu.VMEM((3, NCOL, 2, HR, VX), F32),
        pltpu.VMEM((3, 3, ZS, VX), F32),
        pltpu.VMEM((2, NCOL, WZ, VX), F32),
        pltpu.VMEM((ZS, VX), F32),
        pltpu.VMEM((ZS, VX), F32),
        pltpu.VMEM((ZS, VX), F32),
        pltpu.VMEM((ZS, VX), F32),
        pltpu.VMEM((8, 128), F32),
        pltpu.VMEM((3, flat, 2, 128), F32),
        pltpu.VMEM((3, deep, 2, 128), F32),
        pltpu.VMEM((C, 2 * NA * R), F32),
        dma(()),
        dma((NCOL,)),
        dma((3, NCOL, 2)),
        dma((3, NCOL, 2)),
        dma((3, 3, 2)),
        dma((3, 3, 2)),
        dma((2, NCOL, 2)),
        dma((2, NCOL, 2)),
        dma((2, NCOL, 2)),
        dma((2, NCOL, 2)),
        dma((3, 2)),
        dma((3, 2)),
    ]
    shapes = (
        jax.ShapeDtypeStruct((ZS, VX), F32),
        jax.ShapeDtypeStruct((C, 2 * NA * R), F32),
        jax.ShapeDtypeStruct((ZS, VX), F32),
    )
    outs = pl.pallas_call(
        functools.partial(kernel, lo_size),
        out_shape=shapes,
        in_specs=[smem, smem, vmem, anywhere, anywhere],
        out_specs=(vmem, vmem, vmem),
        scratch_shapes=scratch,
        compiler_params=pltpu.CompilerParams(
            collective_id=0, has_side_effects=True, vmem_limit_bytes=56 * 1024 * 1024
        ),
        cost_estimate=pl.CostEstimate(flops=12_000_000_000, bytes_accessed=9_000_000, transcendentals=0),
    )(view_offset, tile_index, jnp.swapaxes(footprint, 1, 2), measured, transaxial)
    return pl.pallas_call(
        hand_on,
        out_shape=shapes,
        in_specs=[anywhere] * 3,
        out_specs=(anywhere,) * 3,
        scratch_shapes=[pltpu.VMEM(shape.shape, F32) for shape in shapes] + [dma((4,)), dma((4,))],
        compiler_params=pltpu.CompilerParams(vmem_limit_bytes=60 * 1024 * 1024),
    )(*outs)


def solution(mesh):
    lo_size = min(8, mesh.shape["gz"] // 2)
    return jax.shard_map(
        functools.partial(on_device, lo_size),
        mesh=mesh,
        in_specs=(P("col", "gz"), P("gz"), P("gz"), P(), P(None, "col", None)),
        out_specs=(P("gz", "col"), P("col", "gz"), P("gz", "col")),
        check_vma=False,
    )
```

```python
import functools

import jax
import jax.numpy as jnp
from jax import lax
from jax.experimental import pallas as pl
from jax.experimental.pallas import tpu as pltpu
from jax.sharding import PartitionSpec as P

MESH = pl.DeviceIdType.MESH
F32 = jnp.float32
BF16 = jnp.bfloat16

NA = 8
R = 64
ZW = 32
ZS = 128
HR = 64
WZ = 256
C = 184
NXW = 1024
NCOL = 4
VX = NXW // NCOL
PAIRS = NA // 2
PW = 384
KC = PAIRS * PW
TOP = WZ - ZW
SCALE = 2.0**40
NT = (((1,), (1,)), ((), ()))
NN = (((1,), (0,)), ((), ()))


def split(x):
    hi = x.astype(BF16)
    return hi, (x - hi.astype(F32)).astype(BF16)


def dot(a, b, dims):
    return lax.dot_general(a, b, dimension_numbers=dims, preferred_element_type=F32)


def dot3(a_hi, a_lo, b_hi, b_lo, dims):
    a = jnp.concatenate([a_hi, a_lo, a_hi], axis=dims[0][0][0])
    b = jnp.concatenate([b_hi, b_hi, b_lo], axis=dims[0][1][0])
    return dot(a, b, dims)


def squares(x):
    rows, lanes = x.shape
    y = jnp.sum((x * x).reshape(rows // 8, 8, lanes), axis=0)
    return sum(y[:, k * 128 : (k + 1) * 128] for k in range(lanes // 128))


def total(x):
    return jnp.sum(x, axis=(0, 1), keepdims=True)


def kernel(
    lo_size,
    off_ref, tile_ref, foot_ref, measured_ref, trans_ref,
    vol_ref, res_ref, grad_ref,
    stage, t_hi, t_lo, shifted, w_hi, w_lo,
    z_both, q_all, q0, q1, r1,
    part, rim, direct,
    window, g0, g1, h0, h1, scalars,
    ar1, ar2,
    meas_ref, m_sem, t_sem, rim_send, rim_recv, dir_send, dir_recv,
    gat_send, gat_recv, win_send, win_recv, ar_send, ar_recv,
):
    n_gz = lax.axis_size("gz")
    hi_size = n_gz // lo_size
    x_size = lo_size // 2
    gz = lax.axis_index("gz")
    y = lax.axis_index("col")
    z_at = lax.div(gz, lo_size)
    x_at = lax.div(lax.rem(gz, lo_size), 2)
    core = lax.rem(gz, 2)
    inner, outer = 1 - core, core

    def col(d):
        return lax.rem(y + d, NCOL)

    def flat_peer(d):
        at = lax.rem(x_at * NCOL + y + d, x_size * NCOL)
        return (z_at * lo_size + lax.div(at, NCOL) * 2 + core, lax.rem(at, NCOL))

    def deep_peer(d):
        at = lax.rem(z_at * 2 + core + d, hi_size * 2)
        return (lax.div(at, 2) * lo_size + x_at * 2 + lax.rem(at, 2), y)

    groups = ((x_size * NCOL, flat_peer), (hi_size * 2, deep_peer))

    barrier = pltpu.get_barrier_semaphore()

    def greet(to):
        pl.semaphore_signal(barrier, inc=1, device_id=to, device_id_type=MESH)

    def owner(i):
        return lax.rem(y + 2 + 3 * i + 3 * lax.div(i * (i - 1), 2), NCOL)

    def t_load(i):
        cols = pl.ds(pl.multiple_of(owner(i) * VX, VX), VX)
        return pltpu.make_async_copy(trans_ref.at[:, :, cols], stage.at[i], t_sem.at[i])

    loads = [t_load(i) for i in range(NCOL)]
    meas_load = pltpu.make_async_copy(measured_ref, meas_ref, m_sem)
    meas_load.start()
    for load in loads:
        load.start()

    for other in (1, n_gz - 1):
        greet((lax.rem(gz + other, n_gz), y))
        greet((lax.rem(gz + other, n_gz), col(2)))
    for size, peer in groups:
        for d in range(1, size):
            greet(peer(d))
    greeted = groups[0][0] + groups[1][0] + 2

    lane = lax.broadcasted_iota(jnp.int32, (1, 128), 1)
    first_half = lane < 64

    shifted[...] = jnp.zeros_like(shifted)

    def place(a, _):
        shifted[TOP:WZ, :] = jnp.concatenate(
            [foot_ref[tile_ref[a]], foot_ref[tile_ref[a + NA]]], axis=1
        )
        one = shifted[pl.ds(TOP - off_ref[a], WZ), :]
        two = shifted[pl.ds(TOP - off_ref[a + NA], WZ), :]
        hi, lo = split(jnp.where(first_half, one, two))
        w_hi[a] = hi
        w_lo[a] = lo
        return 0

    lax.fori_loop(0, NA, place, 0)

    def z_of(p, x):
        hi, lo = split(x)
        pick = lambda v, k: jnp.concatenate([v[k * 128 : (k + 1) * 128], v[256:]], axis=0)
        za = dot3(w_hi[2 * p], w_lo[2 * p], pick(hi, 0), pick(lo, 0), NT)
        zb = dot3(w_hi[2 * p + 1], w_lo[2 * p + 1], pick(hi, 1), pick(lo, 1), NT)
        third = jnp.where(first_half, za[:, 128:], zb[:, 128:])
        hi, lo = split(jnp.concatenate([za[:, :128], zb[:, :128], third], axis=1))
        at = pl.ds(pl.multiple_of(p * PW, 128), PW)
        z_both[0:WZ, at] = hi
        z_both[WZ:, at] = lo

    def early_at(p):
        return pl.ds(pl.multiple_of(p * 128, 128), 128)

    def late_at(p):
        return pl.ds(pl.multiple_of(NA * R + p * 128, 128), 128)

    def z_of_measured(p, _):
        early = meas_ref[:, early_at(p)]
        late = meas_ref[:, late_at(p)]
        a = jnp.where(first_half, early, pltpu.roll(late, 64, 1))
        b = jnp.where(first_half, pltpu.roll(early, 64, 1), late)
        gap = jnp.zeros((8, 128), F32)
        z_of(p, jnp.concatenate([a[:128], b[:128], a[128:], gap, b[128:], gap], axis=0))
        return 0

    def as_measured(x):
        a = jnp.concatenate([x[0:128], x[256:312]], axis=0)
        b = jnp.concatenate([x[128:256], x[320:376]], axis=0)
        early = jnp.where(first_half, a, pltpu.roll(b, 64, 1))
        late = jnp.where(first_half, pltpu.roll(a, 64, 1), b)
        return early, late

    meas_load.wait()
    lax.fori_loop(0, PAIRS, z_of_measured, 0, unroll=2)

    def convert(i, s):
        t_load(i).wait()

        def some(p, _):
            base = p * PW
            for h in range(2):
                x = stage[i, 2 * p + h]
                hi, lo = split(x[:128])
                at = pl.ds(pl.multiple_of(base + h * 128, 64), 128)
                t_hi[s, at] = hi
                t_lo[s, at] = lo
                hi, lo = split(jnp.concatenate([x[128:], jnp.zeros((8, VX), F32)], axis=0))
                at = pl.ds(pl.multiple_of(base + 256 + h * 64, 64), 64)
                t_hi[s, at] = hi
                t_lo[s, at] = lo
            return 0

        lax.fori_loop(0, PAIRS, some, 0)

    def remote(src, dst, send, recv, to):
        return pltpu.make_async_remote_copy(
            src_ref=src, dst_ref=dst, send_sem=send, recv_sem=recv, device_id=to, device_id_type=MESH
        )

    ar_bufs = (ar1, ar2)
    ar_at = (x_at * NCOL + y, z_at * 2 + core)

    def ar_put(k, level, value):
        size, peer = groups[level]
        slot = ar_bufs[level].at[k, ar_at[level]]
        slot[...] = value
        for d in range(1, size):
            remote(slot, slot, ar_send.at[k, level], ar_recv.at[k, level], peer(d)).start()

    def ar_get(k, level):
        size, peer = groups[level]
        others = ar_bufs[level].at[k, pl.ds(0, size - 1)]
        every = remote(others, others, ar_send.at[k, level], ar_recv.at[k, level], peer(1))
        every.wait_recv()
        every.wait_send()
        return jnp.sum(ar_bufs[level][k], axis=0)

    def ar_first(k, one, two):
        rows = [jnp.sum(v, axis=0, keepdims=True) for v in (one, two)]
        ar_put(k, 0, jnp.concatenate(rows, axis=0))

    def ar_second(k):
        ar_put(k, 1, ar_get(k, 0))

    def half(h, base=HR):
        return pl.ds(pl.multiple_of(base + h * 64, 64), 64)

    def edge(h):
        return pl.ds(pl.multiple_of((1 - h) * (WZ - HR), 64), HR)

    def b_rim(phase, i, h):
        return remote(
            part.at[phase, i, edge(h)], rim.at[phase, i, h],
            rim_send.at[phase, i, h], rim_recv.at[phase, i, h],
            (lax.rem(gz + n_gz + 1 - 2 * h, n_gz), y),
        )

    def b_direct(phase, i, h):
        return remote(
            part.at[phase, i, half(h)], direct.at[phase, i, half(h, 0)],
            dir_send.at[phase, i, h], dir_recv.at[phase, i, h], (gz, owner(i)),
        )

    def with_rim(phase, i, h):
        b_rim(phase, i, h).wait_recv()
        inside = jnp.where(h == 0, gz > 0, gz < n_gz - 1)
        return part[phase, i, half(h)] + jnp.where(inside, rim[phase, i, h], 0.0)

    def send_half(phase, i, h):
        part[phase, i, half(h)] = with_rim(phase, i, h)
        b_direct(phase, i, h).start()

    def back(phase, take, beside1=None, beside2=None):
        def product(i, _):
            s = owner(i)
            if phase == 0:
                convert(i, s)
            both = dot(z_both[...], t_hi[s], NN)
            part[phase, i] = both[0:WZ] + (both[WZ:] + dot(z_both[0:WZ], t_lo[s], NN))
            if phase == 0:

                @pl.when(i == 0)
                def _():
                    pl.semaphore_wait(barrier, greeted)

            b_rim(phase, i, outer).start()
            b_rim(phase, i, inner).start()

            @pl.when(i > 0)
            def _():
                send_half(phase, i - 1, inner)

            return 0

        lax.fori_loop(0, NCOL, product, 0)
        send_half(phase, 0, outer)
        send_half(phase, 1, outer)
        if beside1 is not None:
            beside1()
        send_half(phase, 2, outer)
        if beside2 is not None:
            beside2()
        for h, far in ((inner, False), (outer, True)):
            own = with_rim(phase, 3, h)
            for i in range(3):
                b_direct(phase, i, h).wait_recv()
            d = [direct[phase, i, half(h, 0)] for i in range(3)]
            take(h, own + (d[0] + (d[1] + d[2])), far)

    def a_main(phase, i, h):
        return remote(
            window.at[phase, 0, half(h)], window.at[phase, i, half(h)],
            gat_send.at[phase, i, h], gat_recv.at[phase, i, h],
            (gz, lax.rem(y + i + lax.div(i, 2) + 2 * lax.div(i, 3), NCOL)),
        )

    def a_rim(phase, i, h, far=False):
        src = window.at[phase, 0 if far else i, half(h)]
        return remote(
            src, window.at[phase, i, edge(h)],
            win_send.at[phase, i, h], win_recv.at[phase, i, h],
            (lax.rem(gz + n_gz - 1 + 2 * h, n_gz), col(2) if far else y),
        )

    def gather_start(phase, h, far):
        a_rim(phase, 0, h).start()
        a_main(phase, 1, h).start()
        a_main(phase, 2, h).start()
        if far:
            a_rim(phase, 3, h, True).start()
        a_main(phase, 3, h).start()

    def gather_product(phase, i):
        s = lax.rem(y + 3 * i + 3 * ((i * (i - 1)) // 2), NCOL)
        low = jnp.where(gz > 0, window[phase, i, 0:HR], 0.0)
        high = jnp.where(gz < n_gz - 1, window[phase, i, WZ - HR : WZ], 0.0)
        hi, lo = split(jnp.concatenate([low, window[phase, i, HR : HR + ZS], high], axis=0))

        value = dot3(t_hi[s], t_lo[s], hi, lo, NT)
        if i == 0:
            q_all[...] = value
        else:
            q_all[...] += value

    def gather(phase, beside0=None, beside1=None, beside2=None):
        def product(i):
            for h in range(2):
                a_rim(phase, i, h).wait_recv()
            gather_product(phase, i)

        def forwards(h):
            for i in (1, 2):
                a_main(phase, i, h).wait_recv()
                a_rim(phase, i, h).start()

        forwards(inner)
        if beside0 is not None:
            beside0()
        forwards(outer)
        a_main(phase, 3, inner).wait_recv()
        a_rim(phase, 3, inner).start()
        product(0)
        if beside1 is not None:
            beside1()
        a_main(phase, 3, outer).wait_recv()
        if beside2 is not None:
            beside2()
        product(3)
        product(1)
        product(2)

    def rays(p):
        hi, lo = split(q_all[pl.ds(pl.multiple_of(p * PW, 128), PW)])

        def one(a, k):
            pick = lambda v: jnp.concatenate(
                [v[k * 128 : (k + 1) * 128], v[256 + k * 64 : 320 + k * 64]], axis=0
            )
            both = dot(pick(hi), jnp.concatenate([w_hi[a], w_lo[a]], axis=1), NN)
            return both[:, :128] + (both[:, 128:] + dot(pick(lo), w_hi[a], NN))

        pa = one(2 * p, 0)
        pb = one(2 * p + 1, 1)
        return jnp.concatenate([pa[:128], pb[:128], pa[128:], pb[128:]], axis=0)

    zero8 = jnp.zeros((8, 128), F32)

    def take_g0(h, value, far):
        g0[half(h, 0)] = value
        window[0, 0, half(h)] = value
        gather_start(0, h, far)

    back(0, take_g0)
    gather(0)

    def rays0(p, acc):
        x = rays(p)
        q0[p] = x
        return acc + squares(x)

    def z_of_rays(q):
        lax.fori_loop(0, PAIRS, lambda p, c: (z_of(p, q[p]), c)[1], 0, unroll=4)

    norm_q0 = lax.fori_loop(0, PAIRS, rays0, zero8, unroll=2)
    ar_first(0, squares(g0[...]), norm_q0)
    z_of_rays(q0)

    def take_h0(h, value, far):
        h0[half(h, 0)] = value
        window[1, 0, half(h)] = value * SCALE
        gather_start(1, h, far)

    back(1, take_h0, beside1=lambda: ar_second(0))

    def step0():
        sums = ar_get(0, 1)
        gamma = total(sums[0:1])
        alpha = gamma / total(sums[1:2])
        scalars[0:1] = jnp.broadcast_to(gamma, (1, 128))
        scalars[1:2] = jnp.broadcast_to(alpha, (1, 128))
        g1[...] = g0[...] - alpha * h0[...]
        ar_first(1, squares(g1[...]), zero8)

    gather(1, step0, None, lambda: ar_second(1))
    gamma0 = scalars[0:1, 0:1]
    alpha0 = scalars[1:2, 0:1]

    def rays1(p, _):
        q1[p] = q0[p] - (alpha0 * (1.0 / SCALE)) * rays(p)
        return 0

    lax.fori_loop(0, PAIRS, rays1, 0, unroll=2)

    gamma1 = total(ar_get(1, 1)[0:1])
    beta = gamma1 / gamma0

    def rays2(p, acc):
        x = q1[p] + beta * q0[p]
        q1[p] = x
        return acc + squares(x)

    ar_first(2, lax.fori_loop(0, PAIRS, rays2, zero8), zero8)
    z_of_rays(q1)

    def take_h1(h, value, _):
        h1[half(h, 0)] = value

    def sent_directs(phase):
        for h in range(2):
            for i in range(3):
                b_direct(phase, i, h).wait_send()

    def sent_earlier():
        for phase in range(2):
            sent_directs(phase)
            for h in range(2):
                for i in range(NCOL):
                    a_rim(phase, i, h).wait_send()
                for i in range(1, NCOL):
                    a_main(phase, i, h).wait_send()
        for phase in range(3):
            for h in range(2):
                for i in range(NCOL):
                    b_rim(phase, i, h).wait_send()

    def residual_parts():
        def some(p, _):
            for at, x0, x1 in zip((early_at(p), late_at(p)), as_measured(q0[p]), as_measured(q1[p])):
                r1[:, at] = meas_ref[:, at] - alpha0 * x0
                res_ref[:, at] = x1
            return 0

        lax.fori_loop(0, PAIRS, some, 0)
        sent_earlier()

    back(2, take_h1, beside1=lambda: ar_second(2), beside2=residual_parts)
    sums = ar_get(2, 1)
    alpha1 = gamma1 / total(sums[0:1])
    grad_ref[...] = g1[...] - alpha1 * h1[...]
    vol_ref[...] = alpha0 * g0[...] + alpha1 * (g1[...] + beta * g0[...])
    res_ref[...] = r1[...] - alpha1 * res_ref[...]

    sent_directs(2)


def hand_on(v_ref, r_ref, g_ref, v_out, r_out, g_out, v, r, g, sem_in, sem_out):
    cut = C // 2 // 8 * 8
    pieces = [(r_ref.at[0:cut], r.at[0:cut], r_out.at[0:cut]), (r_ref.at[cut:], r.at[cut:], r_out.at[cut:])]
    pieces += [(v_ref, v, v_out), (g_ref, g, g_out)]
    ins = [pltpu.make_async_copy(a, b, sem_in.at[k]) for k, (a, b, _) in enumerate(pieces)]
    outs = [pltpu.make_async_copy(b, c, sem_out.at[k]) for k, (_, b, c) in enumerate(pieces)]
    for copy in ins:
        copy.start()
    for arrived, copy in zip(ins, outs):
        arrived.wait()
        copy.start()
    for copy in outs:
        copy.wait()


def on_device(lo_size, measured, view_offset, tile_index, footprint, transaxial):
    hi_size = lax.axis_size("gz") // lo_size
    flat, deep = lo_size // 2 * NCOL, hi_size * 2
    vmem = pl.BlockSpec(memory_space=pltpu.VMEM)
    anywhere = pl.BlockSpec(memory_space=pl.ANY)
    smem = pl.BlockSpec(memory_space=pltpu.SMEM)
    dma = pltpu.SemaphoreType.DMA
    scratch = [
        pltpu.VMEM((NCOL, NA, C, VX), F32),
        pltpu.VMEM((NCOL, KC, VX), BF16),
        pltpu.VMEM((NCOL, KC, VX), BF16),
        pltpu.VMEM((TOP + WZ, 128), F32),
        pltpu.VMEM((NA, WZ, 128), BF16),
        pltpu.VMEM((NA, WZ, 128), BF16),
        pltpu.VMEM((2 * WZ, KC), BF16),
        pltpu.VMEM((KC, WZ), F32),
        pltpu.VMEM((PAIRS, PW, 128), F32),
        pltpu.VMEM((PAIRS, PW, 128), F32),
        pltpu.VMEM((C, 2 * NA * R), F32),
        pltpu.VMEM((3, NCOL, WZ, VX), F32),
        pltpu.VMEM((3, NCOL, 2, HR, VX), F32),
        pltpu.VMEM((3, 3, ZS, VX), F32),
        pltpu.VMEM((2, NCOL, WZ, VX), F32),
        pltpu.VMEM((ZS, VX), F32),
        pltpu.VMEM((ZS, VX), F32),
        pltpu.VMEM((ZS, VX), F32),
        pltpu.VMEM((ZS, VX), F32),
        pltpu.VMEM((8, 128), F32),
        pltpu.VMEM((3, flat, 2, 128), F32),
        pltpu.VMEM((3, deep, 2, 128), F32),
        pltpu.VMEM((C, 2 * NA * R), F32),
        dma(()),
        dma((NCOL,)),
        dma((3, NCOL, 2)),
        dma((3, NCOL, 2)),
        dma((3, 3, 2)),
        dma((3, 3, 2)),
        dma((2, NCOL, 2)),
        dma((2, NCOL, 2)),
        dma((2, NCOL, 2)),
        dma((2, NCOL, 2)),
        dma((3, 2)),
        dma((3, 2)),
    ]
    shapes = (
        jax.ShapeDtypeStruct((ZS, VX), F32),
        jax.ShapeDtypeStruct((C, 2 * NA * R), F32),
        jax.ShapeDtypeStruct((ZS, VX), F32),
    )
    outs = pl.pallas_call(
        functools.partial(kernel, lo_size),
        out_shape=shapes,
        in_specs=[smem, smem, vmem, anywhere, anywhere],
        out_specs=(vmem, vmem, vmem),
        scratch_shapes=scratch,
        compiler_params=pltpu.CompilerParams(
            collective_id=0, has_side_effects=True, vmem_limit_bytes=56 * 1024 * 1024
        ),
        cost_estimate=pl.CostEstimate(flops=12_000_000_000, bytes_accessed=9_000_000, transcendentals=0),
    )(view_offset, tile_index, jnp.swapaxes(footprint, 1, 2), measured, transaxial)
    return pl.pallas_call(
        hand_on,
        out_shape=shapes,
        in_specs=[anywhere] * 3,
        out_specs=(anywhere,) * 3,
        scratch_shapes=[pltpu.VMEM(shape.shape, F32) for shape in shapes] + [dma((4,)), dma((4,))],
        compiler_params=pltpu.CompilerParams(vmem_limit_bytes=60 * 1024 * 1024),
    )(*outs)


def solution(mesh):
    lo_size = min(8, mesh.shape["gz"] // 2)
    return jax.shard_map(
        functools.partial(on_device, lo_size),
        mesh=mesh,
        in_specs=(P("col", "gz"), P("gz"), P("gz"), P(), P(None, "col", None)),
        out_specs=(P("gz", "col"), P("col", "gz"), P("gz", "col")),
        check_vma=False,
    )
```

```python
import functools

import jax
import jax.numpy as jnp
from jax import lax
from jax.experimental import pallas as pl
from jax.experimental.pallas import tpu as pltpu
from jax.sharding import PartitionSpec as P

MESH = pl.DeviceIdType.MESH
F32 = jnp.float32
BF16 = jnp.bfloat16

NA = 8
R = 64
ZW = 32
ZS = 128
HR = 64
WZ = 256
C = 184
NXW = 1024
NCOL = 4
VX = NXW // NCOL
PAIRS = NA // 2
PW = 384
KC = PAIRS * PW
TOP = WZ - ZW
SCALE = 2.0**40
NT = (((1,), (1,)), ((), ()))
NN = (((1,), (0,)), ((), ()))


def split(x):
    hi = x.astype(BF16)
    return hi, (x - hi.astype(F32)).astype(BF16)


def dot(a, b, dims):
    return lax.dot_general(a, b, dimension_numbers=dims, preferred_element_type=F32)


def dot3(a_hi, a_lo, b_hi, b_lo, dims):
    a = jnp.concatenate([a_hi, a_lo, a_hi], axis=dims[0][0][0])
    b = jnp.concatenate([b_hi, b_hi, b_lo], axis=dims[0][1][0])
    return dot(a, b, dims)


def squares(x):
    rows, lanes = x.shape
    y = jnp.sum((x * x).reshape(rows // 8, 8, lanes), axis=0)
    return sum(y[:, k * 128 : (k + 1) * 128] for k in range(lanes // 128))


def total(x):
    return jnp.sum(x, axis=(0, 1), keepdims=True)


def kernel(
    lo_size,
    off_ref, tile_ref, foot_ref, measured_ref, trans_ref,
    vol_ref, res_ref, grad_ref,
    stage, t_hi, t_lo, shifted, w_hi, w_lo,
    z_both, q_all, q0, q1, r1,
    part, rim, direct,
    window, g0, g1, h0, h1, scalars,
    ar1, ar2,
    meas_ref, m_sem, t_sem, rim_send, rim_recv, dir_send, dir_recv,
    gat_send, gat_recv, win_send, win_recv, ar_send, ar_recv,
):
    n_gz = lax.axis_size("gz")
    hi_size = n_gz // lo_size
    x_size = lo_size // 2
    gz = lax.axis_index("gz")
    y = lax.axis_index("col")
    z_at = lax.div(gz, lo_size)
    x_at = lax.div(lax.rem(gz, lo_size), 2)
    core = lax.rem(gz, 2)
    inner, outer = 1 - core, core

    def col(d):
        return lax.rem(y + d, NCOL)

    def flat_peer(d):
        at = lax.rem(x_at * NCOL + y + d, x_size * NCOL)
        return (z_at * lo_size + lax.div(at, NCOL) * 2 + core, lax.rem(at, NCOL))

    def deep_peer(d):
        at = lax.rem(z_at * 2 + core + d, hi_size * 2)
        return (lax.div(at, 2) * lo_size + x_at * 2 + lax.rem(at, 2), y)

    groups = ((x_size * NCOL, flat_peer), (hi_size * 2, deep_peer))

    barrier = pltpu.get_barrier_semaphore()

    def greet(to):
        pl.semaphore_signal(barrier, inc=1, device_id=to, device_id_type=MESH)

    def owner(i):
        return lax.rem(y + 2 + 3 * i + 3 * lax.div(i * (i - 1), 2), NCOL)

    def t_load(i):
        cols = pl.ds(pl.multiple_of(owner(i) * VX, VX), VX)
        return pltpu.make_async_copy(trans_ref.at[:, :, cols], stage.at[i], t_sem.at[i])

    loads = [t_load(i) for i in range(NCOL)]
    meas_load = pltpu.make_async_copy(measured_ref, meas_ref, m_sem)
    meas_load.start()
    for load in loads:
        load.start()

    for other in (1, n_gz - 1):
        greet((lax.rem(gz + other, n_gz), y))
        greet((lax.rem(gz + other, n_gz), col(2)))
    for size, peer in groups:
        for d in range(1, size):
            greet(peer(d))
    greeted = groups[0][0] + groups[1][0] + 2

    lane = lax.broadcasted_iota(jnp.int32, (1, 128), 1)
    first_half = lane < 64

    shifted[...] = jnp.zeros_like(shifted)

    def place(a, _):
        shifted[TOP:WZ, :] = jnp.concatenate(
            [foot_ref[tile_ref[a]], foot_ref[tile_ref[a + NA]]], axis=1
        )
        one = shifted[pl.ds(TOP - off_ref[a], WZ), :]
        two = shifted[pl.ds(TOP - off_ref[a + NA], WZ), :]
        hi, lo = split(jnp.where(first_half, one, two))
        w_hi[a] = hi
        w_lo[a] = lo
        return 0

    lax.fori_loop(0, NA, place, 0)

    def z_of(p, x):
        hi, lo = split(x)
        pick = lambda v, k: jnp.concatenate([v[k * 128 : (k + 1) * 128], v[256:]], axis=0)
        za = dot3(w_hi[2 * p], w_lo[2 * p], pick(hi, 0), pick(lo, 0), NT)
        zb = dot3(w_hi[2 * p + 1], w_lo[2 * p + 1], pick(hi, 1), pick(lo, 1), NT)
        third = jnp.where(first_half, za[:, 128:], zb[:, 128:])
        hi, lo = split(jnp.concatenate([za[:, :128], zb[:, :128], third], axis=1))
        at = pl.ds(pl.multiple_of(p * PW, 128), PW)
        z_both[0:WZ, at] = hi
        z_both[WZ:, at] = lo

    def early_at(p):
        return pl.ds(pl.multiple_of(p * 128, 128), 128)

    def late_at(p):
        return pl.ds(pl.multiple_of(NA * R + p * 128, 128), 128)

    def z_of_measured(p, _):
        early = meas_ref[:, early_at(p)]
        late = meas_ref[:, late_at(p)]
        a = jnp.where(first_half, early, pltpu.roll(late, 64, 1))
        b = jnp.where(first_half, pltpu.roll(early, 64, 1), late)
        gap = jnp.zeros((8, 128), F32)
        z_of(p, jnp.concatenate([a[:128], b[:128], a[128:], gap, b[128:], gap], axis=0))
        return 0

    def as_measured(x):
        a = jnp.concatenate([x[0:128], x[256:312]], axis=0)
        b = jnp.concatenate([x[128:256], x[320:376]], axis=0)
        early = jnp.where(first_half, a, pltpu.roll(b, 64, 1))
        late = jnp.where(first_half, pltpu.roll(a, 64, 1), b)
        return early, late

    meas_load.wait()
    lax.fori_loop(0, PAIRS, z_of_measured, 0, unroll=2)

    def convert(i, s):
        t_load(i).wait()

        def some(p, _):
            base = p * PW
            for h in range(2):
                x = stage[i, 2 * p + h]
                hi, lo = split(x[:128])
                at = pl.ds(pl.multiple_of(base + h * 128, 64), 128)
                t_hi[s, at] = hi
                t_lo[s, at] = lo
                hi, lo = split(jnp.concatenate([x[128:], jnp.zeros((8, VX), F32)], axis=0))
                at = pl.ds(pl.multiple_of(base + 256 + h * 64, 64), 64)
                t_hi[s, at] = hi
                t_lo[s, at] = lo
            return 0

        lax.fori_loop(0, PAIRS, some, 0)

    def remote(src, dst, send, recv, to):
        return pltpu.make_async_remote_copy(
            src_ref=src, dst_ref=dst, send_sem=send, recv_sem=recv, device_id=to, device_id_type=MESH
        )

    ar_bufs = (ar1, ar2)
    ar_at = (x_at * NCOL + y, z_at * 2 + core)

    def ar_put(k, level, value):
        size, peer = groups[level]
        slot = ar_bufs[level].at[k, ar_at[level]]
        slot[...] = value
        for d in range(1, size):
            remote(slot, slot, ar_send.at[k, level], ar_recv.at[k, level], peer(d)).start()

    def ar_get(k, level):
        size, peer = groups[level]
        others = ar_bufs[level].at[k, pl.ds(0, size - 1)]
        every = remote(others, others, ar_send.at[k, level], ar_recv.at[k, level], peer(1))
        every.wait_recv()
        every.wait_send()
        return jnp.sum(ar_bufs[level][k], axis=0)

    def ar_first(k, one, two):
        rows = [jnp.sum(v, axis=0, keepdims=True) for v in (one, two)]
        ar_put(k, 0, jnp.concatenate(rows, axis=0))

    def ar_second(k):
        ar_put(k, 1, ar_get(k, 0))

    def half(h, base=HR):
        return pl.ds(pl.multiple_of(base + h * 64, 64), 64)

    def edge(h):
        return pl.ds(pl.multiple_of((1 - h) * (WZ - HR), 64), HR)

    def b_rim(phase, i, h):
        return remote(
            part.at[phase, i, edge(h)], rim.at[phase, i, h],
            rim_send.at[phase, i, h], rim_recv.at[phase, i, h],
            (lax.rem(gz + n_gz + 1 - 2 * h, n_gz), y),
        )

    def b_direct(phase, i, h):
        return remote(
            part.at[phase, i, half(h)], direct.at[phase, i, half(h, 0)],
            dir_send.at[phase, i, h], dir_recv.at[phase, i, h], (gz, owner(i)),
        )

    def with_rim(phase, i, h):
        b_rim(phase, i, h).wait_recv()
        inside = jnp.where(h == 0, gz > 0, gz < n_gz - 1)
        return part[phase, i, half(h)] + jnp.where(inside, rim[phase, i, h], 0.0)

    def send_half(phase, i, h):
        part[phase, i, half(h)] = with_rim(phase, i, h)
        b_direct(phase, i, h).start()

    def back(phase, take, beside1=None, beside2=None):
        def product(i, _):
            s = owner(i)
            if phase == 0:
                convert(i, s)
            both = dot(z_both[...], t_hi[s], NN)
            part[phase, i] = both[0:WZ] + (both[WZ:] + dot(z_both[0:WZ], t_lo[s], NN))
            if phase == 0:

                @pl.when(i == 0)
                def _():
                    pl.semaphore_wait(barrier, greeted)

            b_rim(phase, i, outer).start()
            b_rim(phase, i, inner).start()

            @pl.when(i > 0)
            def _():
                send_half(phase, i - 1, inner)

            return 0

        lax.fori_loop(0, NCOL, product, 0)
        send_half(phase, 0, outer)
        send_half(phase, 1, outer)
        send_half(phase, 2, outer)
        if beside1 is not None:
            beside1()
        if beside2 is not None:
            beside2()
        for h, far in ((inner, False), (outer, True)):
            own = with_rim(phase, 3, h)
            for i in range(3):
                b_direct(phase, i, h).wait_recv()
            d = [direct[phase, i, half(h, 0)] for i in range(3)]
            take(h, own + (d[0] + (d[1] + d[2])), far)

    def a_main(phase, i, h):
        return remote(
            window.at[phase, 0, half(h)], window.at[phase, i, half(h)],
            gat_send.at[phase, i, h], gat_recv.at[phase, i, h],
            (gz, lax.rem(y + i + lax.div(i, 2) + 2 * lax.div(i, 3), NCOL)),
        )

    def a_rim(phase, i, h, far=False):
        src = window.at[phase, 0 if far else i, half(h)]
        return remote(
            src, window.at[phase, i, edge(h)],
            win_send.at[phase, i, h], win_recv.at[phase, i, h],
            (lax.rem(gz + n_gz - 1 + 2 * h, n_gz), col(2) if far else y),
        )

    def gather_start(phase, h, far):
        a_rim(phase, 0, h).start()
        a_main(phase, 1, h).start()
        a_main(phase, 2, h).start()
        if far:
            a_rim(phase, 3, h, True).start()
        a_main(phase, 3, h).start()

    def gather_product(phase, i):
        s = lax.rem(y + 3 * i + 3 * ((i * (i - 1)) // 2), NCOL)
        low = jnp.where(gz > 0, window[phase, i, 0:HR], 0.0)
        high = jnp.where(gz < n_gz - 1, window[phase, i, WZ - HR : WZ], 0.0)
        hi, lo = split(jnp.concatenate([low, window[phase, i, HR : HR + ZS], high], axis=0))

        value = dot3(t_hi[s], t_lo[s], hi, lo, NT)
        if i == 0:
            q_all[...] = value
        else:
            q_all[...] += value

    def gather(phase, beside0=None, beside1=None, beside2=None):
        def product(i):
            for h in range(2):
                a_rim(phase, i, h).wait_recv()
            gather_product(phase, i)

        def forwards(h):
            for i in (1, 2):
                a_main(phase, i, h).wait_recv()
                a_rim(phase, i, h).start()

        forwards(inner)
        if beside0 is not None:
            beside0()
        forwards(outer)
        a_main(phase, 3, inner).wait_recv()
        a_rim(phase, 3, inner).start()
        product(0)
        if beside1 is not None:
            beside1()
        a_main(phase, 3, outer).wait_recv()
        if beside2 is not None:
            beside2()
        product(3)
        product(1)
        product(2)

    def rays(p):
        hi, lo = split(q_all[pl.ds(pl.multiple_of(p * PW, 128), PW)])

        def one(a, k):
            pick = lambda v: jnp.concatenate(
                [v[k * 128 : (k + 1) * 128], v[256 + k * 64 : 320 + k * 64]], axis=0
            )
            both = dot(pick(hi), jnp.concatenate([w_hi[a], w_lo[a]], axis=1), NN)
            return both[:, :128] + (both[:, 128:] + dot(pick(lo), w_hi[a], NN))

        pa = one(2 * p, 0)
        pb = one(2 * p + 1, 1)
        return jnp.concatenate([pa[:128], pb[:128], pa[128:], pb[128:]], axis=0)

    zero8 = jnp.zeros((8, 128), F32)

    def take_g0(h, value, far):
        g0[half(h, 0)] = value
        window[0, 0, half(h)] = value
        gather_start(0, h, far)

    back(0, take_g0)
    gather(0)

    def rays0(p, acc):
        x = rays(p)
        q0[p] = x
        return acc + squares(x)

    def z_of_rays(q):
        lax.fori_loop(0, PAIRS, lambda p, c: (z_of(p, q[p]), c)[1], 0, unroll=4)

    norm_q0 = lax.fori_loop(0, PAIRS, rays0, zero8, unroll=2)
    ar_first(0, squares(g0[...]), norm_q0)
    z_of_rays(q0)

    def take_h0(h, value, far):
        h0[half(h, 0)] = value
        window[1, 0, half(h)] = value * SCALE
        gather_start(1, h, far)

    back(1, take_h0, beside1=lambda: ar_second(0))

    def step0():
        sums = ar_get(0, 1)
        gamma = total(sums[0:1])
        alpha = gamma / total(sums[1:2])
        scalars[0:1] = jnp.broadcast_to(gamma, (1, 128))
        scalars[1:2] = jnp.broadcast_to(alpha, (1, 128))
        g1[...] = g0[...] - alpha * h0[...]
        ar_first(1, squares(g1[...]), zero8)

    gather(1, step0, None, lambda: ar_second(1))
    gamma0 = scalars[0:1, 0:1]
    alpha0 = scalars[1:2, 0:1]

    def rays1(p, _):
        q1[p] = q0[p] - (alpha0 * (1.0 / SCALE)) * rays(p)
        return 0

    lax.fori_loop(0, PAIRS, rays1, 0, unroll=2)

    gamma1 = total(ar_get(1, 1)[0:1])
    beta = gamma1 / gamma0

    def rays2(p, acc):
        x = q1[p] + beta * q0[p]
        q1[p] = x
        return acc + squares(x)

    ar_first(2, lax.fori_loop(0, PAIRS, rays2, zero8), zero8)
    z_of_rays(q1)

    def take_h1(h, value, _):
        h1[half(h, 0)] = value

    def sent_directs(phase):
        for h in range(2):
            for i in range(3):
                b_direct(phase, i, h).wait_send()

    def sent_earlier():
        for phase in range(2):
            sent_directs(phase)
            for h in range(2):
                for i in range(NCOL):
                    a_rim(phase, i, h).wait_send()
                for i in range(1, NCOL):
                    a_main(phase, i, h).wait_send()
        for phase in range(3):
            for h in range(2):
                for i in range(NCOL):
                    b_rim(phase, i, h).wait_send()

    def residual_parts():
        def some(p, _):
            for at, x0, x1 in zip((early_at(p), late_at(p)), as_measured(q0[p]), as_measured(q1[p])):
                r1[:, at] = meas_ref[:, at] - alpha0 * x0
                res_ref[:, at] = x1
            return 0

        lax.fori_loop(0, PAIRS, some, 0)
        sent_earlier()

    back(2, take_h1, beside1=lambda: ar_second(2), beside2=residual_parts)
    sums = ar_get(2, 1)
    alpha1 = gamma1 / total(sums[0:1])
    grad_ref[...] = g1[...] - alpha1 * h1[...]
    vol_ref[...] = alpha0 * g0[...] + alpha1 * (g1[...] + beta * g0[...])
    res_ref[...] = r1[...] - alpha1 * res_ref[...]

    sent_directs(2)


def hand_on(v_ref, r_ref, g_ref, v_out, r_out, g_out, v, r, g, sem_in, sem_out):
    cut = C // 2 // 8 * 8
    pieces = [(r_ref.at[0:cut], r.at[0:cut], r_out.at[0:cut]), (r_ref.at[cut:], r.at[cut:], r_out.at[cut:])]
    pieces += [(v_ref, v, v_out), (g_ref, g, g_out)]
    ins = [pltpu.make_async_copy(a, b, sem_in.at[k]) for k, (a, b, _) in enumerate(pieces)]
    outs = [pltpu.make_async_copy(b, c, sem_out.at[k]) for k, (_, b, c) in enumerate(pieces)]
    for copy in ins:
        copy.start()
    for arrived, copy in zip(ins, outs):
        arrived.wait()
        copy.start()
    for copy in outs:
        copy.wait()


def on_device(lo_size, measured, view_offset, tile_index, footprint, transaxial):
    hi_size = lax.axis_size("gz") // lo_size
    flat, deep = lo_size // 2 * NCOL, hi_size * 2
    vmem = pl.BlockSpec(memory_space=pltpu.VMEM)
    anywhere = pl.BlockSpec(memory_space=pl.ANY)
    smem = pl.BlockSpec(memory_space=pltpu.SMEM)
    dma = pltpu.SemaphoreType.DMA
    scratch = [
        pltpu.VMEM((NCOL, NA, C, VX), F32),
        pltpu.VMEM((NCOL, KC, VX), BF16),
        pltpu.VMEM((NCOL, KC, VX), BF16),
        pltpu.VMEM((TOP + WZ, 128), F32),
        pltpu.VMEM((NA, WZ, 128), BF16),
        pltpu.VMEM((NA, WZ, 128), BF16),
        pltpu.VMEM((2 * WZ, KC), BF16),
        pltpu.VMEM((KC, WZ), F32),
        pltpu.VMEM((PAIRS, PW, 128), F32),
        pltpu.VMEM((PAIRS, PW, 128), F32),
        pltpu.VMEM((C, 2 * NA * R), F32),
        pltpu.VMEM((3, NCOL, WZ, VX), F32),
        pltpu.VMEM((3, NCOL, 2, HR, VX), F32),
        pltpu.VMEM((3, 3, ZS, VX), F32),
        pltpu.VMEM((2, NCOL, WZ, VX), F32),
        pltpu.VMEM((ZS, VX), F32),
        pltpu.VMEM((ZS, VX), F32),
        pltpu.VMEM((ZS, VX), F32),
        pltpu.VMEM((ZS, VX), F32),
        pltpu.VMEM((8, 128), F32),
        pltpu.VMEM((3, flat, 2, 128), F32),
        pltpu.VMEM((3, deep, 2, 128), F32),
        pltpu.VMEM((C, 2 * NA * R), F32),
        dma(()),
        dma((NCOL,)),
        dma((3, NCOL, 2)),
        dma((3, NCOL, 2)),
        dma((3, 3, 2)),
        dma((3, 3, 2)),
        dma((2, NCOL, 2)),
        dma((2, NCOL, 2)),
        dma((2, NCOL, 2)),
        dma((2, NCOL, 2)),
        dma((3, 2)),
        dma((3, 2)),
    ]
    shapes = (
        jax.ShapeDtypeStruct((ZS, VX), F32),
        jax.ShapeDtypeStruct((C, 2 * NA * R), F32),
        jax.ShapeDtypeStruct((ZS, VX), F32),
    )
    outs = pl.pallas_call(
        functools.partial(kernel, lo_size),
        out_shape=shapes,
        in_specs=[smem, smem, vmem, anywhere, anywhere],
        out_specs=(vmem, vmem, vmem),
        scratch_shapes=scratch,
        compiler_params=pltpu.CompilerParams(
            collective_id=0, has_side_effects=True, vmem_limit_bytes=56 * 1024 * 1024
        ),
        cost_estimate=pl.CostEstimate(flops=12_000_000_000, bytes_accessed=9_000_000, transcendentals=0),
    )(view_offset, tile_index, jnp.swapaxes(footprint, 1, 2), measured, transaxial)
    return pl.pallas_call(
        hand_on,
        out_shape=shapes,
        in_specs=[anywhere] * 3,
        out_specs=(anywhere,) * 3,
        scratch_shapes=[pltpu.VMEM(shape.shape, F32) for shape in shapes] + [dma((4,)), dma((4,))],
        compiler_params=pltpu.CompilerParams(vmem_limit_bytes=60 * 1024 * 1024),
    )(*outs)


def solution(mesh):
    lo_size = min(8, mesh.shape["gz"] // 2)
    return jax.shard_map(
        functools.partial(on_device, lo_size),
        mesh=mesh,
        in_specs=(P("col", "gz"), P("gz"), P("gz"), P(), P(None, "col", None)),
        out_specs=(P("gz", "col"), P("col", "gz"), P("gz", "col")),
        check_vma=False,
    )
```
